32 devices in a mesh: seq: 4 (over y, core), space: 8 (over z, x).
Axes of the slice: x: 2, y: 2, z: 4, core: 2. Of those that a mesh axis runs over, the one named last changes fastest.
Arguments:
- features: bfloat16 [2048, 8192], P(None, ('seq', 'space')), may hold values from -6 to 6
- targets: bfloat16 [2048, 8192], P(None, ('seq', 'space')), may hold values from -6 to 6
- write_keys: bfloat16 [128, 8192], P(None, ('seq', 'space')), may hold values from -0.5 to 0.5
- read_queries: bfloat16 [128, 8192], P(None, ('seq', 'space')), may hold values from -0.0625 to 0.0625
- decay_codes: int32 [32, 8192], P('space', 'seq'), may hold values from 0 to 99, as said below
- scan_order: int32 [2048], replicated, may hold values from 0 to 2047, each once
- masked: int32 [6144], P(('seq', 'space')), may hold values from 0 to 8191, as said below
- skip_gain: float32 [32], P('space'), may hold values from 0.5 to 1.5
Outputs:
- mixed: bfloat16 [2048, 8192], P(None, ('seq', 'space'))
- grad_features: bfloat16 [2048, 8192], P(None, ('seq', 'space'))
The draws below stay inside these ranges and needn't reach their ends.
Inputs may be any that keep to these rules, and one draw needn't show every extreme that they name: `decay_codes`: a token's decay factor for its head is exp(-(0.065536 / 8192) code). `masked`: entries k * 192 to (k + 1) * 192 - 1 are distinct indices among tokens k * 256 to (k + 1) * 256 - 1.
All inputs are finite; a program needn't handle non-finite values.
Results may differ from the reference program's by a relative error of at most 0.0034.
Values may be sent and summed in bfloat16 or wider, within the bound.
A program may use at most 128 MiB of HBM per device.

```python
import jax
import jax.numpy as jnp
from jax import lax

HEAD_TOTAL = 32
STATE = 128
TOK_DEV = 256
INNER = 2048
TOK_SEQ = 2048
CLIP_TOKENS = 8192
MASK_DEV = 192


def draw_decay_codes(key, part):
    random_key_speed, random_key_base, random_key_spike, random_key_bigger = jax.random.split(key, 4)
    group_count = CLIP_TOKENS // TOK_SEQ
    ceiling_table = jnp.array([2, 4, 8, 16, 32, 64, 99], jnp.int32)
    ceiling_pick = jax.random.randint(random_key_speed, (HEAD_TOTAL, group_count, 1), 0, 7)
    ceiling = jnp.take(ceiling_table, ceiling_pick)
    shared_default = jax.random.randint(random_key_base, (HEAD_TOTAL, group_count, TOK_SEQ), 0, ceiling)
    shared_default = shared_default.reshape(HEAD_TOTAL, CLIP_TOKENS)
    sudden_spike = jax.random.randint(random_key_spike, (HEAD_TOTAL, CLIP_TOKENS), 0, 256)
    bigger_variant = jax.random.randint(random_key_bigger, (HEAD_TOTAL, CLIP_TOKENS), 80, 100)
    return jnp.where(sudden_spike == 0, bigger_variant, shared_default).astype(jnp.int32)


def draw_masked(key, part):
    groups = CLIP_TOKENS // TOK_DEV
    keys = jax.random.split(key, groups)
    picks = jax.vmap(lambda sub_key: jax.random.permutation(sub_key, TOK_DEV)[:MASK_DEV])(keys)
    offsets = jnp.arange(groups, dtype=jnp.int32)[:, None] * TOK_DEV
    return (picks.astype(jnp.int32) + offsets).reshape(-1).astype(jnp.int32)


def shard_levels(own_key, extent, cuts, low, top_value):
    factor_of = 1.0
    for dim, parts in cuts:
        draws = jax.random.uniform(jax.random.fold_in(jax.random.fold_in(own_key, 6), dim), (parts,), jnp.float32, low / len(cuts), top_value / len(cuts))
        factor_of = factor_of * jnp.repeat(jnp.exp(draws), extent[dim] // parts).reshape((-1,) + (1,) * (len(extent) - 1 - dim))
    return factor_of


def gaussian(key, extent, scale, limit, cuts=(), held_as=jnp.bfloat16):
    values = scale * jax.random.normal(key, extent, jnp.float32)
    if cuts:
        values = values * shard_levels(key, extent, cuts, -0.22, 0.18)
    return jnp.clip(values, -limit, limit).astype(held_as)


def setup_inputs(seed: int = 0) -> dict:
    arg_keys = jax.random.split(jax.random.key(seed), 9)
    features = gaussian(arg_keys[0], (INNER, CLIP_TOKENS), 1.0, 6.0, ((1, 32),))
    targets = gaussian(arg_keys[1], (INNER, CLIP_TOKENS), 1.0, 6.0, ((1, 32),))
    write_keys = gaussian(arg_keys[2], (STATE, CLIP_TOKENS), STATE ** -0.5, 0.5, ((1, 32),))
    read_queries = gaussian(arg_keys[3], (STATE, CLIP_TOKENS), CLIP_TOKENS ** -0.5, 0.0625, ((1, 32),))
    decay_codes = draw_decay_codes(jax.random.fold_in(arg_keys[8], 71), 0)
    scan_order = jax.random.permutation(arg_keys[5], TOK_SEQ).astype(jnp.int32)
    masked = draw_masked(jax.random.fold_in(arg_keys[8], 71), 0)
    skip_gain = jnp.clip(0.5 + 1.0 * jax.random.uniform(arg_keys[7], (HEAD_TOTAL,), jnp.float32) ** shard_levels(arg_keys[7], (HEAD_TOTAL,), ((0, 8),), -0.2, 0.2), 0.5, 1.5)
    return {"features": features, "targets": targets, "write_keys": write_keys, "read_queries": read_queries, "decay_codes": decay_codes, "scan_order": scan_order, "masked": masked, "skip_gain": skip_gain}


highest = lax.Precision.HIGHEST


def fading(amount):
    return jnp.exp(-(0.065536 / CLIP_TOKENS) * amount.astype(jnp.float32))


def mix_head(values, into_state, from_state, running, block_size):
    head_width, length = values.shape
    state_count = into_state.shape[0]
    block_count = length // block_size
    value_blocks = values.reshape(head_width, block_count, block_size).transpose(1, 0, 2)
    into_blocks = into_state.reshape(state_count, block_count, block_size).transpose(1, 0, 2)
    from_blocks = from_state.reshape(state_count, block_count, block_size).transpose(1, 0, 2)
    step_blocks = running.reshape(block_count, block_size)
    starting = jnp.concatenate([jnp.zeros((1,), jnp.int32), step_blocks[:-1, -1].astype(jnp.int32)])
    zero_state = jnp.zeros((state_count, head_width), jnp.float32)

    def forward_blocks(state_sum, pieces):
        value_block, into_block, from_block, step_block, earlier = pieces
        latest = step_block[-1]
        gram_block = jnp.dot(into_block.T, from_block, precision=highest)
        weights = (gram_block * fading(jnp.abs(step_block[None, :] - step_block[:, None]))).astype(jnp.bfloat16)
        inside = jnp.dot(value_block.astype(jnp.bfloat16), weights, preferred_element_type=jnp.float32).astype(jnp.float32)
        readout = jnp.dot(state_sum.T, from_block * fading(step_block - earlier)[None, :], precision=highest)
        update = jnp.dot(into_block * fading(latest - step_block)[None, :], value_block.T, precision=highest)
        return state_sum * fading(latest - earlier) + update, inside + readout

    def reverse_blocks(state_sum, pieces):
        value_block, into_block, from_block, step_block, earlier = pieces
        latest = step_block[-1]
        readout = jnp.dot(state_sum.T, from_block * fading(latest - step_block)[None, :], precision=highest)
        update = jnp.dot(into_block * fading(step_block - earlier)[None, :], value_block.T, precision=highest)
        return state_sum * fading(latest - earlier) + update, readout

    sequence = (value_blocks, into_blocks, from_blocks, step_blocks, starting)
    forward_out = lax.scan(forward_blocks, zero_state, sequence)[1]
    reverse_out = lax.scan(reverse_blocks, zero_state, sequence, reverse=True)[1]
    return (forward_out + reverse_out).transpose(1, 0, 2).reshape(head_width, length)


def reference(features, targets, write_keys, read_queries, decay_codes, scan_order, masked, skip_gain):
    inner, tokens = features.shape
    head_count = decay_codes.shape[0]
    head_width = inner // head_count
    seq_share = scan_order.shape[0]
    position = (jnp.arange(tokens // seq_share, dtype=jnp.int32)[:, None] * seq_share + scan_order[None, :].astype(jnp.int32)).reshape(-1).astype(jnp.int32)
    undo = jnp.zeros((tokens,), jnp.int32).at[position].set(jnp.arange(tokens, dtype=jnp.int32))
    block_size = min(512, seq_share)
    into_state = write_keys.astype(jnp.float32)[:, position]
    from_state = read_queries.astype(jnp.float32)[:, position]
    running = jnp.cumsum(decay_codes[:, position], axis=1).astype(jnp.int32)
    per_head = features.reshape(head_count, head_width, tokens)

    def forward_head(triple):
        values = triple[0].astype(jnp.float32)[:, position]
        return mix_head(values, into_state, from_state, triple[1], block_size) + triple[2] * values

    mixed_scan = lax.map(forward_head, (per_head, running, skip_gain))
    mixed = mixed_scan.reshape(inner, tokens)[:, undo].astype(jnp.bfloat16)
    mask_row = jnp.zeros((tokens,), jnp.float32).at[masked].set(1.0)
    residue = (mask_row[None, :] * (mixed.astype(jnp.float32) - targets.astype(jnp.float32))).astype(jnp.bfloat16)
    residue_heads = residue.reshape(head_count, head_width, tokens)

    def backward_head(triple):
        values = triple[0].astype(jnp.float32)[:, position]
        return mix_head(values, from_state, into_state, triple[1], block_size) + triple[2] * values

    grads_scan = lax.map(backward_head, (residue_heads, running, skip_gain))
    grad_features = grads_scan.reshape(inner, tokens)[:, undo].astype(jnp.bfloat16)
    return mixed, grad_features
```

```python
from functools import partial

import jax
import jax.numpy as jnp
from jax import lax
from jax.experimental import pallas as pl
from jax.experimental.pallas import tpu as pltpu
from jax.sharding import PartitionSpec as P

MESH = pl.DeviceIdType.MESH
F32 = jnp.float32
BF16 = jnp.bfloat16


def dot(a, b):
    return jnp.dot(a, b, preferred_element_type=F32)


def dot_nt(a, b):
    return lax.dot_general(a, b, (((1,), (1,)), ((), ())), preferred_element_type=F32)


def xor(n, me, i):
    out, m = 0, 1
    while m < n:
        x, y = (me // m) % 2, (i // m) % 2
        out = out + m * (x + y - 2 * x * y)
        m *= 2
    return out


def kernel(
    nsp, nsq, heads, unit,
    feat, targ, keys, codes, order, gain,
    mixed_o, grad_o,
    x_s, t_s, slab, xa, xb, mix_s, grad_s, pan_m, pan_n, w_t, q_t, rank_c, rank_r, codes_f, a_s, b_s,
    tot_s, tot_r, st_s, st_r, bst, ast,
    key_ss, key_rs, x_ss, x_rs, t_ss, t_rs, m_ss, m_rs, g_ss, g_rs, tot_ss, tot_rs, st_ss, st_rs,
):
    me, mine = lax.axis_index("space"), lax.axis_index("seq")
    tok = feat.shape[1]
    rows = feat.shape[0] // nsp
    state = w_t.shape[1]
    width = rows // heads

    def chunk(i):
        return pl.ds(pl.multiple_of(i * tok, tok), tok)

    def part(i):
        return pl.ds(pl.multiple_of(i * rows, rows), rows)

    def to_space(src, dst, ss, rs, c):
        return pltpu.make_async_remote_copy(
            src_ref=src, dst_ref=dst, send_sem=ss.at[c], recv_sem=rs.at[c],
            device_id={"space": xor(nsp, me, c)}, device_id_type=MESH,
        )

    def to_seq(src, dst, ss, rs, c):
        return pltpu.make_async_remote_copy(
            src_ref=src, dst_ref=dst, send_sem=ss.at[c], recv_sem=rs.at[c],
            device_id={"seq": xor(nsq, mine, c)}, device_id_type=MESH,
        )

    barrier = pltpu.get_barrier_semaphore()
    for c in range(1, nsp):
        pl.semaphore_signal(barrier, inc=1, device_id={"space": xor(nsp, me, c)}, device_id_type=MESH)
    for c in range(1, nsq):
        pl.semaphore_signal(barrier, inc=1, device_id={"seq": xor(nsq, mine, c)}, device_id_type=MESH)
    slab[me] = keys[...]
    codes_f[...] = jnp.zeros_like(codes_f)
    codes_f[0:heads, :] = codes[...].astype(F32)
    tot_s[...] = jnp.broadcast_to(jnp.sum(codes_f[...], axis=1, keepdims=True), tot_s.shape)
    pl.semaphore_wait(barrier, nsp + nsq - 2)

    def key_copy(m, c):
        place = xor(nsp, me, c)
        return pltpu.make_async_remote_copy(
            src_ref=slab.at[place], dst_ref=slab.at[place], send_sem=key_ss.at[m + c],
            recv_sem=key_rs.at[m + c], device_id={"space": xor(nsp, me, m)}, device_id_type=MESH,
        )

    key_copies = {}

    def key_step(m):
        held = range(0, nsp, 2 * m)
        for c in held:
            if c % (4 * m):
                key_copies[c].wait_recv()
        for c in held:
            key_copies[m + c] = key_copy(m, c)
            key_copies[m + c].start()

    key_step(nsp // 2)
    tot_copies = [to_seq(tot_s, tot_r.at[c], tot_ss, tot_rs, c) for c in range(1, nsq)]
    for copy in tot_copies:
        copy.start()
    x_copies = {
        c: to_space(feat.at[part(xor(nsp, me, c)), :], x_s.at[me], x_ss, x_rs, c) for c in range(1, nsp)
    }
    for c in reversed(range(1, nsp)):
        x_copies[c].start()
    x_s[me] = feat[part(me), :]

    length = nsp * tok
    places = lax.broadcasted_iota(jnp.int32, (tok, length), 1).astype(F32)

    def rank_chunk(i, carry):
        token = lax.broadcasted_iota(jnp.int32, (tok, length), 0) + i * tok
        rank = jnp.sum(jnp.where(order[...] == token, places, 0.0), axis=1, keepdims=True)
        wide = jnp.broadcast_to(rank, (tok, 128))
        rank_c[chunk(i), :] = wide
        rank_r[i] = jnp.transpose(wide)[0:8, :]
        return carry

    lax.fori_loop(0, nsp, rank_chunk, 0)

    def before(j, k):
        col = rank_c[chunk(j), :]
        return jnp.concatenate([col] * (tok // 128), axis=1) <= rank_r[k][0:1, :]

    m = nsp // 4
    key_step(m)

    for copy in tot_copies:
        copy.wait_recv()
    offset = jnp.zeros(tot_s.shape, F32)
    for c in range(1, nsq):
        offset = offset + jnp.where(xor(nsq, mine, c) < mine, tot_r[c], 0.0)

    def run_chunk(k, carry):
        def add(j, acc):
            return acc + dot(
                codes_f[:, chunk(j)].astype(BF16), jnp.where(before(j, k), 1.0, 0.0).astype(BF16)
            )

        run = lax.fori_loop(0, nsp, add, jnp.broadcast_to(offset[:, 0:1], (codes_f.shape[0], tok)))
        a_s[k] = jnp.exp(-unit * run)
        b_s[k] = jnp.exp(unit * run)
        return carry

    lax.fori_loop(0, nsp, run_chunk, 0)

    while m > 1:
        m //= 2
        key_step(m)
    for c in range(1, nsp, 2):
        key_copies[c].wait_recv()

    def flip(i, carry):
        w_t[chunk(i), :] = jnp.transpose(slab[i, 0:state, :].astype(F32)).astype(BF16)
        q_t[chunk(i), :] = jnp.transpose(slab[i, state : 2 * state, :].astype(F32)).astype(BF16)
        return carry

    lax.fori_loop(0, nsp, flip, 0)

    def spread(ref, k):
        t = ref[k]
        return jnp.concatenate(
            [jnp.broadcast_to(t[h : h + 1, :], (width, tok)) for h in range(heads)], axis=0
        )

    def take_chunk(j, sums, side):
        value = x_s[j].astype(F32)
        va, vb = (value * spread(a_s, j)).astype(BF16), (value * spread(b_s, j)).astype(BF16)
        xa[:, chunk(j)] = va
        xb[:, chunk(j)] = vb
        into = slab[j, side : side + state, :]
        return sums[0] + dot_nt(vb, into), sums[1] + dot_nt(va, into)

    none = (jnp.zeros((rows, state), F32), jnp.zeros((rows, state), F32))

    def send_states(turn, sums):
        st_s[turn, 0] = sums[0].astype(BF16)
        st_s[turn, 1] = sums[1].astype(BF16)
        copies = []
        for c in range(1, nsq):
            there = xor(nsq, mine, c)
            which = (nsq + mine - there) // nsq
            copies.append(
                to_seq(
                    st_s.at[turn, which], st_r.at[turn, c], st_ss.at[turn], st_rs.at[turn], c
                )
            )
            copies[-1].start()
        return copies

    def take_states(turn, copies):
        early, late = jnp.zeros((rows, state), F32), jnp.zeros((rows, state), F32)
        for c in range(1, nsq):
            copies[c - 1].wait_recv()
            got = st_r[turn, c].astype(F32)
            there = xor(nsq, mine, c)
            early = early + jnp.where(there < mine, got, 0.0)
            late = late + jnp.where(there > mine, got, 0.0)
        bst[...] = early.astype(BF16)
        ast[...] = late.astype(BF16)

    def mix_chunk(k, into_t, side):
        from_k = slab[k, side : side + state, :]

        def panel(j, carry):
            gram = dot(into_t[chunk(j), :], from_k)
            ahead = before(j, k)
            pan_m[chunk(j), :] = jnp.where(ahead, gram, 0.0).astype(BF16)
            pan_n[chunk(j), :] = jnp.where(ahead, 0.0, gram).astype(BF16)
            return carry

        lax.fori_loop(0, nsp, panel, 0)
        out = spread(a_s, k) * (dot(xb[...], pan_m[...]) + dot(bst[...], from_k))
        out = out + spread(b_s, k) * (dot(xa[...], pan_n[...]) + dot(ast[...], from_k))
        value = x_s[k].astype(F32)
        skip = jnp.concatenate(
            [value[h * width : (h + 1) * width, :] * gain[h] for h in range(heads)], axis=0
        )
        return (out + skip).astype(BF16)

    sums = take_chunk(me, none, 0)
    for c in range(1, nsp):
        x_copies[c].wait_recv()
    t_copies = {
        c: to_space(targ.at[part(xor(nsp, me, c)), :], t_s.at[me], t_ss, t_rs, c) for c in range(1, nsp)
    }
    for c in reversed(range(1, nsp)):
        t_copies[c].start()
    t_s[me] = targ[part(me), :]
    sums = lax.fori_loop(1, nsp, lambda c, s: take_chunk(xor(nsp, me, c), s, 0), sums)
    states = send_states(0, sums)
    take_states(0, states)

    def forward(k, carry):
        mix_s[k] = mix_chunk(k, w_t, state)
        return carry

    lax.fori_loop(0, nsp, forward, 0)

    m_copies = {
        c: to_space(mix_s.at[xor(nsp, me, c)], mixed_o.at[part(me), :], m_ss, m_rs, c)
        for c in range(1, nsp)
    }
    for c in range(1, nsp):
        t_copies[c].wait_recv()
    for c in reversed(range(1, nsp)):
        m_copies[c].start()
    mixed_o[part(me), :] = mix_s[me]

    def residue(j, sums):
        keep = slab[j, 2 * state : 2 * state + 16, :].astype(F32)[0:1, :]
        x_s[j] = (keep * (mix_s[j].astype(F32) - t_s[j].astype(F32))).astype(BF16)
        return take_chunk(j, sums, state)

    sums = lax.fori_loop(0, nsp, residue, none)
    grad_states = send_states(1, sums)
    take_states(1, grad_states)

    def grad_copy(c):
        return to_space(grad_s.at[xor(nsp, me, c)], grad_o.at[part(me), :], g_ss, g_rs, c)

    def backward(i, carry):
        c = nsp - 1 - i
        grad_s[xor(nsp, me, c)] = mix_chunk(xor(nsp, me, c), q_t, 0)

        @pl.when(c > 0)
        def _():
            grad_copy(c).start()

        return carry

    lax.fori_loop(0, nsp, backward, 0)
    grad_o[part(me), :] = grad_s[me]

    for c in range(1, nsp):
        key_copies[c].wait_send()
        x_copies[c].wait_send()
        t_copies[c].wait_send()
    for copies in (tot_copies, states, grad_states):
        for copy in copies:
            copy.wait_send()
    for c in range(1, nsp):
        m_copies[c].wait()
        grad_copy(c).wait()


def per_device(
    features, targets, write_keys, read_queries, decay_codes, scan_order, masked, skip_gain
):
    nsp, nsq = lax.axis_size("space"), lax.axis_size("seq")
    heads = decay_codes.shape[0]
    inner, tok = features.shape
    state = write_keys.shape[0]
    length = nsp * tok
    rows = inner // nsp
    unit = 0.065536 / (length * nsq)
    first_token = (lax.axis_index("seq") * nsp + lax.axis_index("space")) * tok
    slot_grid = lax.broadcasted_iota(jnp.int32, (masked.shape[0], tok), 1)
    mask_row = jnp.max(
        jnp.where((masked - first_token)[:, None] == slot_grid, 1.0, 0.0), axis=0
    ).astype(BF16)
    keys = jnp.concatenate(
        [write_keys, read_queries, jnp.broadcast_to(mask_row[None], (16, tok))], axis=0
    )
    hp = 16 * (-(-heads // 16))
    vmem = pl.BlockSpec(memory_space=pltpu.VMEM)
    dma = pltpu.SemaphoreType.DMA
    return pl.pallas_call(
        partial(kernel, nsp, nsq, heads, unit),
        out_shape=(
            jax.ShapeDtypeStruct((inner, tok), BF16), jax.ShapeDtypeStruct((inner, tok), BF16)
        ),
        in_specs=[vmem] * 5 + [pl.BlockSpec(memory_space=pltpu.SMEM)],
        out_specs=(vmem, vmem),
        scratch_shapes=[
            pltpu.VMEM((nsp, rows, tok), BF16),
            pltpu.VMEM((nsp, rows, tok), BF16),
            pltpu.VMEM((nsp, 2 * state + 16, tok), BF16),
            pltpu.VMEM((rows, length), BF16),
            pltpu.VMEM((rows, length), BF16),
            pltpu.VMEM((nsp, rows, tok), BF16),
            pltpu.VMEM((nsp, rows, tok), BF16),
            pltpu.VMEM((length, tok), BF16),
            pltpu.VMEM((length, tok), BF16),
            pltpu.VMEM((length, state), BF16),
            pltpu.VMEM((length, state), BF16),
            pltpu.VMEM((length, 128), F32),
            pltpu.VMEM((nsp, 8, tok), F32),
            pltpu.VMEM((hp, length), F32),
            pltpu.VMEM((nsp, hp, tok), F32),
            pltpu.VMEM((nsp, hp, tok), F32),
            pltpu.VMEM((hp, 128), F32),
            pltpu.VMEM((nsq, hp, 128), F32),
            pltpu.VMEM((2, 2, rows, state), BF16),
            pltpu.VMEM((2, nsq, rows, state), BF16),
            pltpu.VMEM((rows, state), BF16),
            pltpu.VMEM((rows, state), BF16),
            *[dma((nsp,)) for _ in range(10)],
            dma((nsq,)), dma((nsq,)),
            dma((2, nsq)), dma((2, nsq)),
        ],
        compiler_params=pltpu.CompilerParams(
            collective_id=0, has_side_effects=True, vmem_limit_bytes=56 * 1024 * 1024
        ),
    )(features, targets, keys, decay_codes, scan_order.reshape(1, length), skip_gain)


def solution(mesh):
    return jax.shard_map(
        per_device,
        mesh=mesh,
        in_specs=(
            P(None, ("seq", "space")),
            P(None, ("seq", "space")),
            P(None, ("seq", "space")),
            P(None, ("seq", "space")),
            P("space", "seq"),
            P(),
            P(("seq", "space")),
            P("space"),
        ),
        out_specs=(P(None, ("seq", "space")), P(None, ("seq", "space"))),
        check_vma=False,
    )
```

```python
from functools import partial

import jax
import jax.numpy as jnp
from jax import lax
from jax.experimental import pallas as pl
from jax.experimental.pallas import tpu as pltpu
from jax.sharding import PartitionSpec as P

MESH = pl.DeviceIdType.MESH
F32 = jnp.float32
BF16 = jnp.bfloat16


def dot(a, b):
    return jnp.dot(a, b, preferred_element_type=F32)


def dot_nt(a, b):
    return lax.dot_general(a, b, (((1,), (1,)), ((), ())), preferred_element_type=F32)


def xor(n, me, i):
    out, m = 0, 1
    while m < n:
        x, y = (me // m) % 2, (i // m) % 2
        out = out + m * (x + y - 2 * x * y)
        m *= 2
    return out


def kernel(
    nsp, nsq, heads, unit,
    feat, targ, keys, codes, order, gain,
    mixed_o, grad_o,
    x_s, t_s, slab, xa, xb, mix_s, grad_s, pan_m, pan_n, w_t, q_t, rank_c, rank_r, codes_f, a_s, b_s,
    tot_s, tot_r, st_s, st_r, bst, ast,
    key_ss, key_rs, x_ss, x_rs, t_ss, t_rs, m_ss, m_rs, g_ss, g_rs, tot_ss, tot_rs, st_ss, st_rs,
):
    me, mine = lax.axis_index("space"), lax.axis_index("seq")
    tok = feat.shape[1]
    rows = feat.shape[0] // nsp
    state = w_t.shape[1]
    width = rows // heads

    def chunk(i):
        return pl.ds(pl.multiple_of(i * tok, tok), tok)

    def part(i):
        return pl.ds(pl.multiple_of(i * rows, rows), rows)

    def to_space(src, dst, ss, rs, c):
        return pltpu.make_async_remote_copy(
            src_ref=src, dst_ref=dst, send_sem=ss.at[c], recv_sem=rs.at[c],
            device_id={"space": xor(nsp, me, c)}, device_id_type=MESH,
        )

    def to_seq(src, dst, ss, rs, c):
        return pltpu.make_async_remote_copy(
            src_ref=src, dst_ref=dst, send_sem=ss.at[c], recv_sem=rs.at[c],
            device_id={"seq": xor(nsq, mine, c)}, device_id_type=MESH,
        )

    barrier = pltpu.get_barrier_semaphore()
    for c in range(1, nsp):
        pl.semaphore_signal(barrier, inc=1, device_id={"space": xor(nsp, me, c)}, device_id_type=MESH)
    for c in range(1, nsq):
        pl.semaphore_signal(barrier, inc=1, device_id={"seq": xor(nsq, mine, c)}, device_id_type=MESH)
    slab[me] = keys[...]
    codes_f[...] = jnp.zeros_like(codes_f)
    codes_f[0:heads, :] = codes[...].astype(F32)
    tot_s[...] = jnp.broadcast_to(jnp.sum(codes_f[...], axis=1, keepdims=True), tot_s.shape)
    pl.semaphore_wait(barrier, nsp + nsq - 2)

    def key_copy(m, c):
        place = xor(nsp, me, c)
        return pltpu.make_async_remote_copy(
            src_ref=slab.at[place], dst_ref=slab.at[place], send_sem=key_ss.at[m + c],
            recv_sem=key_rs.at[m + c], device_id={"space": xor(nsp, me, m)}, device_id_type=MESH,
        )

    key_copies = {}

    def key_step(m):
        held = range(0, nsp, 2 * m)
        for c in held:
            if c % (4 * m):
                key_copies[c].wait_recv()
        for c in held:
            key_copies[m + c] = key_copy(m, c)
            key_copies[m + c].start()

    key_step(nsp // 2)
    tot_copies = [to_seq(tot_s, tot_r.at[c], tot_ss, tot_rs, c) for c in range(1, nsq)]
    for copy in tot_copies:
        copy.start()
    x_copies = {
        c: to_space(feat.at[part(xor(nsp, me, c)), :], x_s.at[me], x_ss, x_rs, c) for c in range(1, nsp)
    }
    for c in range(1, nsp // 2):
        x_copies[c].start()
    x_s[me] = feat[part(me), :]

    length = nsp * tok
    places = lax.broadcasted_iota(jnp.int32, (tok, length), 1).astype(F32)

    def rank_chunk(i, carry):
        token = lax.broadcasted_iota(jnp.int32, (tok, length), 0) + i * tok
        rank = jnp.sum(jnp.where(order[...] == token, places, 0.0), axis=1, keepdims=True)
        wide = jnp.broadcast_to(rank, (tok, 128))
        rank_c[chunk(i), :] = wide
        rank_r[i] = jnp.transpose(wide)[0:8, :]
        return carry

    lax.fori_loop(0, nsp, rank_chunk, 0)

    def before(j, k):
        col = rank_c[chunk(j), :]
        return jnp.concatenate([col] * (tok // 128), axis=1) <= rank_r[k][0:1, :]

    m = nsp // 4
    key_step(m)
    for c in reversed(range(nsp // 2, nsp)):
        x_copies[c].start()

    for copy in tot_copies:
        copy.wait_recv()
    offset = jnp.zeros(tot_s.shape, F32)
    for c in range(1, nsq):
        offset = offset + jnp.where(xor(nsq, mine, c) < mine, tot_r[c], 0.0)

    def run_chunk(k, carry):
        def add(j, acc):
            return acc + dot(
                codes_f[:, chunk(j)].astype(BF16), jnp.where(before(j, k), 1.0, 0.0).astype(BF16)
            )

        run = lax.fori_loop(0, nsp, add, jnp.broadcast_to(offset[:, 0:1], (codes_f.shape[0], tok)))
        a_s[k] = jnp.exp(-unit * run)
        b_s[k] = jnp.exp(unit * run)
        return carry

    lax.fori_loop(0, nsp, run_chunk, 0)

    while m > 1:
        m //= 2
        key_step(m)
    for c in range(1, nsp, 2):
        key_copies[c].wait_recv()

    def flip(i, carry):
        w_t[chunk(i), :] = jnp.transpose(slab[i, 0:state, :].astype(F32)).astype(BF16)
        q_t[chunk(i), :] = jnp.transpose(slab[i, state : 2 * state, :].astype(F32)).astype(BF16)
        return carry

    lax.fori_loop(0, nsp, flip, 0)

    def spread(ref, k):
        t = ref[k]
        return jnp.concatenate(
            [jnp.broadcast_to(t[h : h + 1, :], (width, tok)) for h in range(heads)], axis=0
        )

    def take_chunk(j, sums, side):
        value = x_s[j].astype(F32)
        ta, tb = value * spread(a_s, j), value * spread(b_s, j)
        va, vb = ta.astype(BF16), tb.astype(BF16)
        xa[:, chunk(j)] = va
        xb[:, chunk(j)] = vb
        into = slab[j, side : side + state, :]
        la, lb = (ta - va.astype(F32)).astype(BF16), (tb - vb.astype(F32)).astype(BF16)
        return (
            sums[0] + (dot_nt(vb, into) + dot_nt(lb, into)),
            sums[1] + (dot_nt(va, into) + dot_nt(la, into)),
        )

    none = (jnp.zeros((rows, state), F32), jnp.zeros((rows, state), F32))

    def send_states(turn, sums):
        st_s[turn, 0] = sums[0]
        st_s[turn, 1] = sums[1]
        copies = []
        for c in range(1, nsq):
            there = xor(nsq, mine, c)
            which = (nsq + mine - there) // nsq
            copies.append(
                to_seq(
                    st_s.at[turn, which], st_r.at[turn, c], st_ss.at[turn], st_rs.at[turn], c
                )
            )
            copies[-1].start()
        return copies

    def take_states(turn, copies):
        early, late = jnp.zeros((rows, state), F32), jnp.zeros((rows, state), F32)
        for c in range(1, nsq):
            copies[c - 1].wait_recv()
            got = st_r[turn, c]
            there = xor(nsq, mine, c)
            early = early + jnp.where(there < mine, got, 0.0)
            late = late + jnp.where(there > mine, got, 0.0)
        for ref, total in ((bst, early), (ast, late)):
            high = total.astype(BF16)
            ref[0] = high
            ref[1] = (total - high.astype(F32)).astype(BF16)

    def mix_chunk(k, into_t, side):
        from_k = slab[k, side : side + state, :]

        def panel(j, carry):
            gram = dot(into_t[chunk(j), :], from_k)
            ahead = before(j, k)
            pan_m[chunk(j), :] = jnp.where(ahead, gram, 0.0).astype(BF16)
            pan_n[chunk(j), :] = jnp.where(ahead, 0.0, gram).astype(BF16)
            return carry

        lax.fori_loop(0, nsp, panel, 0)
        out = spread(a_s, k) * (dot(xb[...], pan_m[...]) + (dot(bst[0], from_k) + dot(bst[1], from_k)))
        out = out + spread(b_s, k) * (dot(xa[...], pan_n[...]) + (dot(ast[0], from_k) + dot(ast[1], from_k)))
        value = x_s[k].astype(F32)
        skip = jnp.concatenate(
            [value[h * width : (h + 1) * width, :] * gain[h] for h in range(heads)], axis=0
        )
        return (out + skip).astype(BF16)

    sums = take_chunk(me, none, 0)
    t_copies = {
        c: to_space(targ.at[part(xor(nsp, me, c)), :], t_s.at[me], t_ss, t_rs, c) for c in range(1, nsp)
    }
    for c in reversed(range(1, nsp)):
        x_copies[c].wait_send()
        t_copies[c].start()
    for c in range(1, nsp):
        x_copies[c].wait_recv()
    t_s[me] = targ[part(me), :]
    sums = lax.fori_loop(1, nsp, lambda c, s: take_chunk(xor(nsp, me, c), s, 0), sums)
    states = send_states(0, sums)
    take_states(0, states)

    def mixed_copy(c):
        return to_space(mix_s.at[xor(nsp, me, c)], mixed_o.at[part(me), :], m_ss, m_rs, c)

    def forward(i, carry):
        c = nsp - 1 - i
        mix_s[xor(nsp, me, c)] = mix_chunk(xor(nsp, me, c), w_t, state)

        @pl.when(c > 0)
        def _():
            mixed_copy(c).start()

        return carry

    lax.fori_loop(0, nsp, forward, 0)
    for c in range(1, nsp):
        t_copies[c].wait_recv()
    mixed_o[part(me), :] = mix_s[me]

    def residue(j, sums):
        keep = slab[j, 2 * state : 2 * state + 16, :].astype(F32)[0:1, :]
        x_s[j] = (keep * (mix_s[j].astype(F32) - t_s[j].astype(F32))).astype(BF16)
        return take_chunk(j, sums, state)

    sums = lax.fori_loop(0, nsp, residue, none)
    grad_states = send_states(1, sums)
    take_states(1, grad_states)

    def grad_copy(c):
        return to_space(grad_s.at[xor(nsp, me, c)], grad_o.at[part(me), :], g_ss, g_rs, c)

    def backward(i, carry):
        c = nsp - 1 - i
        grad_s[xor(nsp, me, c)] = mix_chunk(xor(nsp, me, c), q_t, 0)

        @pl.when(c > 0)
        def _():
            grad_copy(c).start()

        return carry

    lax.fori_loop(0, nsp, backward, 0)
    grad_o[part(me), :] = grad_s[me]

    for c in range(1, nsp):
        key_copies[c].wait_send()
        t_copies[c].wait_send()
    for copies in (tot_copies, states, grad_states):
        for copy in copies:
            copy.wait_send()
    for c in range(1, nsp):
        mixed_copy(c).wait()
        grad_copy(c).wait()


def per_device(
    features, targets, write_keys, read_queries, decay_codes, scan_order, masked, skip_gain
):
    nsp, nsq = lax.axis_size("space"), lax.axis_size("seq")
    heads = decay_codes.shape[0]
    inner, tok = features.shape
    state = write_keys.shape[0]
    length = nsp * tok
    rows = inner // nsp
    unit = 0.065536 / (length * nsq)
    first_token = (lax.axis_index("seq") * nsp + lax.axis_index("space")) * tok
    slot_grid = lax.broadcasted_iota(jnp.int32, (masked.shape[0], tok), 1)
    mask_row = jnp.max(
        jnp.where((masked - first_token)[:, None] == slot_grid, 1.0, 0.0), axis=0
    ).astype(BF16)
    keys = jnp.concatenate(
        [write_keys, read_queries, jnp.broadcast_to(mask_row[None], (16, tok))], axis=0
    )
    hp = 16 * (-(-heads // 16))
    vmem = pl.BlockSpec(memory_space=pltpu.VMEM)
    dma = pltpu.SemaphoreType.DMA
    return pl.pallas_call(
        partial(kernel, nsp, nsq, heads, unit),
        out_shape=(
            jax.ShapeDtypeStruct((inner, tok), BF16), jax.ShapeDtypeStruct((inner, tok), BF16)
        ),
        in_specs=[vmem] * 5 + [pl.BlockSpec(memory_space=pltpu.SMEM)],
        out_specs=(vmem, vmem),
        scratch_shapes=[
            pltpu.VMEM((nsp, rows, tok), BF16),
            pltpu.VMEM((nsp, rows, tok), BF16),
            pltpu.VMEM((nsp, 2 * state + 16, tok), BF16),
            pltpu.VMEM((rows, length), BF16),
            pltpu.VMEM((rows, length), BF16),
            pltpu.VMEM((nsp, rows, tok), BF16),
            pltpu.VMEM((nsp, rows, tok), BF16),
            pltpu.VMEM((length, tok), BF16),
            pltpu.VMEM((length, tok), BF16),
            pltpu.VMEM((length, state), BF16),
            pltpu.VMEM((length, state), BF16),
            pltpu.VMEM((length, 128), F32),
            pltpu.VMEM((nsp, 8, tok), F32),
            pltpu.VMEM((hp, length), F32),
            pltpu.VMEM((nsp, hp, tok), F32),
            pltpu.VMEM((nsp, hp, tok), F32),
            pltpu.VMEM((hp, 128), F32),
            pltpu.VMEM((nsq, hp, 128), F32),
            pltpu.VMEM((2, 2, rows, state), F32),
            pltpu.VMEM((2, nsq, rows, state), F32),
            pltpu.VMEM((2, rows, state), BF16),
            pltpu.VMEM((2, rows, state), BF16),
            *[dma((nsp,)) for _ in range(10)],
            dma((nsq,)), dma((nsq,)),
            dma((2, nsq)), dma((2, nsq)),
        ],
        compiler_params=pltpu.CompilerParams(
            collective_id=0, has_side_effects=True, vmem_limit_bytes=56 * 1024 * 1024
        ),
    )(features, targets, keys, decay_codes, scan_order.reshape(1, length), skip_gain)


def solution(mesh):
    return jax.shard_map(
        per_device,
        mesh=mesh,
        in_specs=(
            P(None, ("seq", "space")),
            P(None, ("seq", "space")),
            P(None, ("seq", "space")),
            P(None, ("seq", "space")),
            P("space", "seq"),
            P(),
            P(("seq", "space")),
            P("space"),
        ),
        out_specs=(P(None, ("seq", "space")), P(None, ("seq", "space"))),
        check_vma=False,
    )
```

```python
from functools import partial

import jax
import jax.numpy as jnp
from jax import lax
from jax.experimental import pallas as pl
from jax.experimental.pallas import tpu as pltpu
from jax.sharding import PartitionSpec as P

MESH = pl.DeviceIdType.MESH
F32 = jnp.float32
BF16 = jnp.bfloat16


def dot(a, b):
    return jnp.dot(a, b, preferred_element_type=F32)


def dot_nt(a, b):
    return lax.dot_general(a, b, (((1,), (1,)), ((), ())), preferred_element_type=F32)


def xor(n, me, i):
    out, m = 0, 1
    while m < n:
        x, y = (me // m) % 2, (i // m) % 2
        out = out + m * (x + y - 2 * x * y)
        m *= 2
    return out


def kernel(
    nsp, nsq, heads, unit,
    feat, targ, write, read, codes, order, masked, gain,
    mixed_o, grad_o,
    x_s, t_s, t_p, slab, xa, xb, mix_s, grad_s, pan_m, pan_n, w_t, q_t, rank_c, rank_r, codes_f, a_s, b_s,
    tot_s, tot_r, st_s, st_r, bst, ast,
    key_ss, key_rs, x_ss, x_rs, t_ss, t_rs, m_ss, m_rs, g_ss, g_rs, tot_ss, tot_rs, st_ss, st_rs,
):
    me, mine = lax.axis_index("space"), lax.axis_index("seq")
    tok = feat.shape[1]
    rows = feat.shape[0] // nsp
    state = w_t.shape[1]
    width = rows // heads

    def chunk(i):
        return pl.ds(pl.multiple_of(i * tok, tok), tok)

    def part(i):
        return pl.ds(pl.multiple_of(i * rows, rows), rows)

    def to_space(src, dst, ss, rs, c):
        return pltpu.make_async_remote_copy(
            src_ref=src, dst_ref=dst, send_sem=ss.at[c], recv_sem=rs.at[c],
            device_id={"space": xor(nsp, me, c)}, device_id_type=MESH,
        )

    def to_seq(src, dst, ss, rs, c):
        return pltpu.make_async_remote_copy(
            src_ref=src, dst_ref=dst, send_sem=ss.at[c], recv_sem=rs.at[c],
            device_id={"seq": xor(nsq, mine, c)}, device_id_type=MESH,
        )

    barrier = pltpu.get_barrier_semaphore()
    for c in range(1, nsp):
        pl.semaphore_signal(barrier, inc=1, device_id={"space": xor(nsp, me, c)}, device_id_type=MESH)
    for c in range(1, nsq):
        pl.semaphore_signal(barrier, inc=1, device_id={"seq": xor(nsq, mine, c)}, device_id_type=MESH)
    slab[me, 0:state, :] = write[...]
    slab[me, state : 2 * state, :] = read[...]
    token = lax.broadcasted_iota(jnp.int32, (tok, masked.shape[1]), 0) + (mine * nsp + me) * tok
    hit = jnp.max(jnp.where(masked[...] == token, 1.0, 0.0), axis=1, keepdims=True)
    hit = jnp.transpose(jnp.broadcast_to(hit, (tok, 128)))[0:16, :]
    slab[me, 2 * state : 2 * state + 16, :] = hit.astype(BF16)
    codes_f[...] = jnp.zeros_like(codes_f)
    codes_f[0:heads, :] = codes[...].astype(F32)
    tot_s[...] = jnp.broadcast_to(jnp.sum(codes_f[...], axis=1, keepdims=True), tot_s.shape)
    pl.semaphore_wait(barrier, nsp + nsq - 2)

    def key_copy(m, c):
        place = xor(nsp, me, c)
        return pltpu.make_async_remote_copy(
            src_ref=slab.at[place], dst_ref=slab.at[place], send_sem=key_ss.at[m + c],
            recv_sem=key_rs.at[m + c], device_id={"space": xor(nsp, me, m)}, device_id_type=MESH,
        )

    key_copies = {}

    def key_step(m):
        held = range(0, nsp, 2 * m)
        for c in held:
            if c % (4 * m):
                key_copies[c].wait_recv()
        for c in held:
            key_copies[m + c] = key_copy(m, c)
            key_copies[m + c].start()

    key_step(nsp // 2)
    tot_copies = [to_seq(tot_s, tot_r.at[c], tot_ss, tot_rs, c) for c in range(1, nsq)]
    for copy in tot_copies:
        copy.start()
    x_copies = {
        c: to_space(feat.at[part(xor(nsp, me, c)), :], x_s.at[me], x_ss, x_rs, c) for c in range(1, nsp)
    }
    for c in range(1, nsp // 2):
        x_copies[c].start()
    x_s[me] = feat[part(me), :]

    length = nsp * tok
    places = lax.broadcasted_iota(jnp.int32, (tok, length), 1).astype(F32)

    def rank_chunk(i, carry):
        token = lax.broadcasted_iota(jnp.int32, (tok, length), 0) + i * tok
        rank = jnp.sum(jnp.where(order[...] == token, places, 0.0), axis=1, keepdims=True)
        wide = jnp.broadcast_to(rank, (tok, 128))
        rank_c[chunk(i), :] = wide
        rank_r[i] = jnp.transpose(wide)[0:8, :]
        return carry

    lax.fori_loop(0, nsp, rank_chunk, 0)

    def picks(j):
        keep = slab[j, 2 * state : 2 * state + 16, :]
        older = lax.broadcasted_iota(jnp.int32, (tok, tok), 0) <= lax.broadcasted_iota(
            jnp.int32, (tok, tok), 1
        )
        count = dot(keep, jnp.where(older, 1.0, 0.0).astype(BF16))[0:1, :]
        slot = lax.broadcasted_iota(jnp.int32, (masked.shape[1], tok), 0).astype(F32) + 1.0
        return jnp.where(count == slot, keep.astype(F32)[0:1, :], 0.0).astype(BF16)

    def before(j, k):
        col = rank_c[chunk(j), :]
        return jnp.concatenate([col] * (tok // 128), axis=1) <= rank_r[k][0:1, :]

    m = nsp // 4
    key_step(m)
    for c in reversed(range(nsp // 2, nsp)):
        x_copies[c].start()

    def pack(d, carry):
        t_p[d] = dot_nt(picks(me), targ[part(d), :]).astype(BF16)
        return carry

    lax.fori_loop(0, nsp, pack, 0)

    for copy in tot_copies:
        copy.wait_recv()
    offset = jnp.zeros(tot_s.shape, F32)
    for c in range(1, nsq):
        offset = offset + jnp.where(xor(nsq, mine, c) < mine, tot_r[c], 0.0)

    def run_chunk(k, carry):
        def add(j, acc):
            return acc + dot(
                codes_f[:, chunk(j)].astype(BF16), jnp.where(before(j, k), 1.0, 0.0).astype(BF16)
            )

        run = lax.fori_loop(0, nsp, add, jnp.broadcast_to(offset[:, 0:1], (codes_f.shape[0], tok)))
        a_s[k] = jnp.exp(-unit * run)
        b_s[k] = jnp.exp(unit * run)
        return carry

    lax.fori_loop(0, nsp, run_chunk, 0)

    while m > 1:
        m //= 2
        key_step(m)
    for c in range(1, nsp, 2):
        key_copies[c].wait_recv()

    def flip(i, carry):
        w_t[chunk(i), :] = jnp.transpose(slab[i, 0:state, :].astype(F32)).astype(BF16)
        q_t[chunk(i), :] = jnp.transpose(slab[i, state : 2 * state, :].astype(F32)).astype(BF16)
        return carry

    lax.fori_loop(0, nsp, flip, 0)

    def spread(ref, k):
        t = ref[k]
        return jnp.concatenate(
            [jnp.broadcast_to(t[h : h + 1, :], (width, tok)) for h in range(heads)], axis=0
        )

    def take_chunk(j, sums, side):
        value = x_s[j].astype(F32)
        ta, tb = value * spread(a_s, j), value * spread(b_s, j)
        va, vb = ta.astype(BF16), tb.astype(BF16)
        xa[:, chunk(j)] = va
        xb[:, chunk(j)] = vb
        into = slab[j, side : side + state, :]
        la, lb = (ta - va.astype(F32)).astype(BF16), (tb - vb.astype(F32)).astype(BF16)
        return (
            sums[0] + (dot_nt(vb, into) + dot_nt(lb, into)),
            sums[1] + (dot_nt(va, into) + dot_nt(la, into)),
        )

    none = (jnp.zeros((rows, state), F32), jnp.zeros((rows, state), F32))

    def send_states(turn, sums):
        st_s[turn, 0] = sums[0]
        st_s[turn, 1] = sums[1]
        copies = []
        for c in range(1, nsq):
            there = xor(nsq, mine, c)
            which = (nsq + mine - there) // nsq
            copies.append(
                to_seq(
                    st_s.at[turn, which], st_r.at[turn, c], st_ss.at[turn], st_rs.at[turn], c
                )
            )
            copies[-1].start()
        return copies

    def take_states(turn, copies):
        early, late = jnp.zeros((rows, state), F32), jnp.zeros((rows, state), F32)
        for c in range(1, nsq):
            copies[c - 1].wait_recv()
            got = st_r[turn, c]
            there = xor(nsq, mine, c)
            early = early + jnp.where(there < mine, got, 0.0)
            late = late + jnp.where(there > mine, got, 0.0)
        for ref, total in ((bst, early), (ast, late)):
            high = total.astype(BF16)
            ref[0] = high
            ref[1] = (total - high.astype(F32)).astype(BF16)

    def mix_chunk(k, into_t, side):
        from_k = slab[k, side : side + state, :]

        def panel(j, carry):
            gram = dot(into_t[chunk(j), :], from_k)
            ahead = before(j, k)
            pan_m[chunk(j), :] = jnp.where(ahead, gram, 0.0).astype(BF16)
            pan_n[chunk(j), :] = jnp.where(ahead, 0.0, gram).astype(BF16)
            return carry

        lax.fori_loop(0, nsp, panel, 0)
        out = spread(a_s, k) * (dot(xb[...], pan_m[...]) + (dot(bst[0], from_k) + dot(bst[1], from_k)))
        out = out + spread(b_s, k) * (dot(xa[...], pan_n[...]) + (dot(ast[0], from_k) + dot(ast[1], from_k)))
        value = x_s[k].astype(F32)
        skip = jnp.concatenate(
            [value[h * width : (h + 1) * width, :] * gain[h] for h in range(heads)], axis=0
        )
        return (out + skip).astype(BF16)

    sums = take_chunk(me, none, 0)
    t_copies = {
        c: to_space(t_p.at[xor(nsp, me, c)], t_s.at[me], t_ss, t_rs, c) for c in range(1, nsp)
    }
    for c in reversed(range(1, nsp)):
        x_copies[c].wait_send()
        t_copies[c].start()
    for c in range(1, nsp):
        x_copies[c].wait_recv()
    t_s[me] = t_p[me]
    sums = lax.fori_loop(1, nsp, lambda c, s: take_chunk(xor(nsp, me, c), s, 0), sums)
    states = send_states(0, sums)
    take_states(0, states)

    def mixed_copy(c):
        return to_space(mix_s.at[xor(nsp, me, c)], mixed_o.at[part(me), :], m_ss, m_rs, c)

    def forward(i, carry):
        c = nsp - 1 - i
        mix_s[xor(nsp, me, c)] = mix_chunk(xor(nsp, me, c), w_t, state)

        @pl.when(c > 0)
        def _():
            mixed_copy(c).start()

        return carry

    lax.fori_loop(0, nsp, forward, 0)
    for c in range(1, nsp):
        t_copies[c].wait_recv()
    mixed_o[part(me), :] = mix_s[me]

    def residue(j, sums):
        keep = slab[j, 2 * state : 2 * state + 16, :].astype(F32)[0:1, :]
        wanted = lax.dot_general(
            t_s[j], picks(j), (((0,), (0,)), ((), ())), preferred_element_type=F32
        )
        x_s[j] = (keep * (mix_s[j].astype(F32) - wanted)).astype(BF16)
        return take_chunk(j, sums, state)

    sums = lax.fori_loop(0, nsp, residue, none)
    grad_states = send_states(1, sums)
    take_states(1, grad_states)

    def grad_copy(c):
        return to_space(grad_s.at[xor(nsp, me, c)], grad_o.at[part(me), :], g_ss, g_rs, c)

    def backward(i, carry):
        c = nsp - 1 - i
        grad_s[xor(nsp, me, c)] = mix_chunk(xor(nsp, me, c), q_t, 0)

        @pl.when(c > 0)
        def _():
            grad_copy(c).start()

        return carry

    lax.fori_loop(0, nsp, backward, 0)
    grad_o[part(me), :] = grad_s[me]

    for c in range(1, nsp):
        key_copies[c].wait_send()
        t_copies[c].wait_send()
    for copies in (tot_copies, states, grad_states):
        for copy in copies:
            copy.wait_send()
    for c in range(1, nsp):
        mixed_copy(c).wait()
        grad_copy(c).wait()


def per_device(
    features, targets, write_keys, read_queries, decay_codes, scan_order, masked, skip_gain
):
    nsp, nsq = lax.axis_size("space"), lax.axis_size("seq")
    heads = decay_codes.shape[0]
    inner, tok = features.shape
    state = write_keys.shape[0]
    length = nsp * tok
    rows = inner // nsp
    unit = 0.065536 / (length * nsq)
    hp = 16 * (-(-heads // 16))
    vmem = pl.BlockSpec(memory_space=pltpu.VMEM)
    dma = pltpu.SemaphoreType.DMA
    return pl.pallas_call(
        partial(kernel, nsp, nsq, heads, unit),
        out_shape=(
            jax.ShapeDtypeStruct((inner, tok), BF16), jax.ShapeDtypeStruct((inner, tok), BF16)
        ),
        in_specs=[vmem] * 7 + [pl.BlockSpec(memory_space=pltpu.SMEM)],
        out_specs=(vmem, vmem),
        scratch_shapes=[
            pltpu.VMEM((nsp, rows, tok), BF16),
            pltpu.VMEM((nsp, masked.shape[0], rows), BF16),
            pltpu.VMEM((nsp, masked.shape[0], rows), BF16),
            pltpu.VMEM((nsp, 2 * state + 16, tok), BF16),
            pltpu.VMEM((rows, length), BF16),
            pltpu.VMEM((rows, length), BF16),
            pltpu.VMEM((nsp, rows, tok), BF16),
            pltpu.VMEM((nsp, rows, tok), BF16),
            pltpu.VMEM((length, tok), BF16),
            pltpu.VMEM((length, tok), BF16),
            pltpu.VMEM((length, state), BF16),
            pltpu.VMEM((length, state), BF16),
            pltpu.VMEM((length, 128), F32),
            pltpu.VMEM((nsp, 8, tok), F32),
            pltpu.VMEM((hp, length), F32),
            pltpu.VMEM((nsp, hp, tok), F32),
            pltpu.VMEM((nsp, hp, tok), F32),
            pltpu.VMEM((hp, 128), F32),
            pltpu.VMEM((nsq, hp, 128), F32),
            pltpu.VMEM((2, 2, rows, state), F32),
            pltpu.VMEM((2, nsq, rows, state), F32),
            pltpu.VMEM((2, rows, state), BF16),
            pltpu.VMEM((2, rows, state), BF16),
            *[dma((nsp,)) for _ in range(10)],
            dma((nsq,)), dma((nsq,)),
            dma((2, nsq)), dma((2, nsq)),
        ],
        compiler_params=pltpu.CompilerParams(
            collective_id=0, has_side_effects=True, vmem_limit_bytes=56 * 1024 * 1024
        ),
    )(
        features, targets, write_keys, read_queries, decay_codes,
        scan_order.reshape(1, length), masked.reshape(1, masked.shape[0]), skip_gain,
    )


def solution(mesh):
    return jax.shard_map(
        per_device,
        mesh=mesh,
        in_specs=(
            P(None, ("seq", "space")),
            P(None, ("seq", "space")),
            P(None, ("seq", "space")),
            P(None, ("seq", "space")),
            P("space", "seq"),
            P(),
            P(("seq", "space")),
            P("space"),
        ),
        out_specs=(P(None, ("seq", "space")), P(None, ("seq", "space"))),
        check_vma=False,
    )
```

```python
from functools import partial

import jax
import jax.numpy as jnp
from jax import lax
from jax.experimental import pallas as pl
from jax.experimental.pallas import tpu as pltpu
from jax.sharding import PartitionSpec as P

MESH = pl.DeviceIdType.MESH
F32 = jnp.float32
BF16 = jnp.bfloat16


def dot(a, b):
    return jnp.dot(a, b, preferred_element_type=F32)


def dot_nt(a, b):
    return lax.dot_general(a, b, (((1,), (1,)), ((), ())), preferred_element_type=F32)


def xor(n, me, i):
    out, m = 0, 1
    while m < n:
        x, y = (me // m) % 2, (i // m) % 2
        out = out + m * (x + y - 2 * x * y)
        m *= 2
    return out


def kernel(
    nsp, nsq, heads, unit,
    feat, targ, write, read, codes, order, masked, gain,
    mixed_o, grad_o,
    x_s, t_s, t_p, slab, xab, mix_s, grad_s, gm_c, gm_r, w_t, q_t, rank_c, rank_r, codes_f, a_s, b_s,
    tot_s, tot_r, st_s, st_r, sab,
    key_ss, key_rs, x_ss, x_rs, t_ss, t_rs, m_ss, m_rs, g_ss, g_rs, tot_ss, tot_rs, st_ss, st_rs,
):
    me, mine = lax.axis_index("space"), lax.axis_index("seq")
    tok = feat.shape[1]
    rows = feat.shape[0] // nsp
    state = w_t.shape[1]
    width = rows // heads

    def chunk(i):
        return pl.ds(pl.multiple_of(i * tok, tok), tok)

    def part(i):
        return pl.ds(pl.multiple_of(i * rows, rows), rows)

    def to_space(src, dst, ss, rs, c):
        return pltpu.make_async_remote_copy(
            src_ref=src, dst_ref=dst, send_sem=ss.at[c], recv_sem=rs.at[c],
            device_id={"space": xor(nsp, me, c)}, device_id_type=MESH,
        )

    def to_seq(src, dst, ss, rs, c):
        return pltpu.make_async_remote_copy(
            src_ref=src, dst_ref=dst, send_sem=ss.at[c], recv_sem=rs.at[c],
            device_id={"seq": xor(nsq, mine, c)}, device_id_type=MESH,
        )

    barrier = pltpu.get_barrier_semaphore()
    for c in range(1, nsp):
        pl.semaphore_signal(barrier, inc=1, device_id={"space": xor(nsp, me, c)}, device_id_type=MESH)
    for c in range(1, nsq):
        pl.semaphore_signal(barrier, inc=1, device_id={"seq": xor(nsq, mine, c)}, device_id_type=MESH)
    slab[me, 0:state, :] = write[...]
    slab[me, state : 2 * state, :] = read[...]
    token = lax.broadcasted_iota(jnp.int32, (tok, masked.shape[1]), 0) + (mine * nsp + me) * tok
    hit = jnp.max(jnp.where(masked[...] == token, 1.0, 0.0), axis=1, keepdims=True)
    hit = jnp.transpose(jnp.broadcast_to(hit, (tok, 128)))[0:16, :]
    slab[me, 2 * state : 2 * state + 16, :] = hit.astype(BF16)
    codes_f[...] = jnp.zeros_like(codes_f)
    codes_f[0:heads, :] = codes[...].astype(F32)
    tot_s[...] = jnp.broadcast_to(jnp.sum(codes_f[...], axis=1, keepdims=True), tot_s.shape)
    pl.semaphore_wait(barrier, nsp + nsq - 2)

    def key_copy(m, c):
        place = xor(nsp, me, c)
        return pltpu.make_async_remote_copy(
            src_ref=slab.at[place], dst_ref=slab.at[place], send_sem=key_ss.at[m + c],
            recv_sem=key_rs.at[m + c], device_id={"space": xor(nsp, me, m)}, device_id_type=MESH,
        )

    key_copies = {}

    def key_step(m):
        held = range(0, nsp, 2 * m)
        for c in held:
            if c % (4 * m):
                key_copies[c].wait_recv()
        for c in held:
            key_copies[m + c] = key_copy(m, c)
            key_copies[m + c].start()

    key_step(nsp // 2)
    tot_copies = [to_seq(tot_s, tot_r.at[c], tot_ss, tot_rs, c) for c in range(1, nsq)]
    for copy in tot_copies:
        copy.start()
    x_copies = {
        c: to_space(feat.at[part(xor(nsp, me, c)), :], x_s.at[me], x_ss, x_rs, c) for c in range(1, nsp)
    }
    for c in range(1, nsp // 2):
        x_copies[c].start()
    x_s[me] = feat[part(me), :]

    length = nsp * tok
    places = lax.broadcasted_iota(jnp.int32, (tok, length), 1).astype(F32)

    def rank_chunk(i, carry):
        token = lax.broadcasted_iota(jnp.int32, (tok, length), 0) + i * tok
        rank = jnp.sum(jnp.where(order[...] == token, places, 0.0), axis=1, keepdims=True)
        wide = jnp.broadcast_to(rank, (tok, 128))
        rank_c[chunk(i), :] = wide
        rank_r[i] = jnp.transpose(wide)[0:8, :]
        return carry

    lax.fori_loop(0, nsp, rank_chunk, 0)

    def picks(j):
        keep = slab[j, 2 * state : 2 * state + 16, :]
        older = lax.broadcasted_iota(jnp.int32, (tok, tok), 0) <= lax.broadcasted_iota(
            jnp.int32, (tok, tok), 1
        )
        count = dot(keep, jnp.where(older, 1.0, 0.0).astype(BF16))[0:1, :]
        slot = lax.broadcasted_iota(jnp.int32, (masked.shape[1], tok), 0).astype(F32) + 1.0
        return jnp.where(count == slot, keep.astype(F32)[0:1, :], 0.0).astype(BF16)

    def before(j, k):
        col = rank_c[chunk(j), :]
        return jnp.concatenate([col] * (tok // 128), axis=1) <= rank_r[k][0:1, :]

    m = nsp // 4
    key_step(m)
    for c in reversed(range(nsp // 2, nsp)):
        x_copies[c].start()

    def pack(d, carry):
        t_p[d] = dot_nt(picks(me), targ[part(d), :]).astype(BF16)
        return carry

    lax.fori_loop(0, nsp, pack, 0)

    for copy in tot_copies:
        copy.wait_recv()
    offset = jnp.zeros(tot_s.shape, F32)
    for c in range(1, nsq):
        offset = offset + jnp.where(xor(nsq, mine, c) < mine, tot_r[c], 0.0)

    def run_chunk(k, carry):
        def add(j, acc):
            return acc + dot(
                codes_f[:, chunk(j)].astype(BF16), jnp.where(before(j, k), 1.0, 0.0).astype(BF16)
            )

        run = lax.fori_loop(0, nsp, add, jnp.broadcast_to(offset[:, 0:1], (codes_f.shape[0], tok)))
        a_s[k] = jnp.exp(-unit * run)
        b_s[k] = jnp.exp(unit * run)
        return carry

    lax.fori_loop(0, nsp, run_chunk, 0)

    while m > 1:
        m //= 2
        key_step(m)
    for c in range(1, nsp, 2):
        key_copies[c].wait_recv()

    def flip(i, carry):
        w_t[chunk(i), :] = jnp.transpose(slab[i, 0:state, :].astype(F32)).astype(BF16)
        q_t[chunk(i), :] = jnp.transpose(slab[i, state : 2 * state, :].astype(F32)).astype(BF16)
        return carry

    lax.fori_loop(0, nsp, flip, 0)

    def spread(ref, k):
        t = ref[k]
        return jnp.concatenate(
            [jnp.broadcast_to(t[h : h + 1, :], (width, tok)) for h in range(heads)], axis=0
        )

    def gram(j, k):
        tile = dot(w_t[chunk(j), :], slab[k, state : 2 * state, :])
        return jnp.where(before(j, k), tile, 0.0).astype(BF16)

    whole = gm_c.shape[1] == length

    def columns(k):
        if whole:
            return gm_c[:, chunk(k)]

        def fill(j, carry):
            gm_c[chunk(j), :] = gram(j, k)
            return carry

        lax.fori_loop(0, nsp, fill, 0)
        return gm_c[...]

    def lines(j):
        if whole:
            return gm_c[chunk(j), :]

        def fill(k, carry):
            gm_r[:, chunk(k)] = gram(j, k)
            return carry

        lax.fori_loop(0, nsp, fill, 0)
        return gm_r[...]

    if whole:

        def fill_all(j, carry):
            def fill(k, carry):
                gm_c[chunk(j), chunk(k)] = gram(j, k)
                return carry

            return lax.fori_loop(0, nsp, fill, carry)

        lax.fori_loop(0, nsp, fill_all, 0)

    def take_chunk(j, sums, into_t):
        value = x_s[j].astype(F32)
        wide = jnp.concatenate([value * spread(b_s, j), value * spread(a_s, j)], axis=0)
        high = wide.astype(BF16)
        low = (wide - high.astype(F32)).astype(BF16)
        xab[:, chunk(j)] = high
        into = into_t[chunk(j), :]
        return sums + (dot(high, into) + dot(low, into))

    none = jnp.zeros((2 * rows, state), F32)

    def send_states(turn, sums):
        st_s[turn, 0] = sums[0:rows]
        st_s[turn, 1] = sums[rows : 2 * rows]
        copies = []
        for c in range(1, nsq):
            there = xor(nsq, mine, c)
            which = (nsq + mine - there) // nsq
            copies.append(
                to_seq(
                    st_s.at[turn, which], st_r.at[turn, c], st_ss.at[turn], st_rs.at[turn], c
                )
            )
            copies[-1].start()
        return copies

    def take_states(turn, copies, own):
        totals = [jnp.zeros((rows, state), F32), jnp.zeros((rows, state), F32)]
        totals[own] = st_s[turn, own]
        for c in range(1, nsq):
            copies[c - 1].wait_recv()
            got = st_r[turn, c]
            there = xor(nsq, mine, c)
            totals[0] = totals[0] + jnp.where(there < mine, got, 0.0)
            totals[1] = totals[1] + jnp.where(there > mine, got, 0.0)
        for i in range(2):
            high = totals[i].astype(BF16)
            sab[i * rows : (i + 1) * rows, 0:state] = high
            sab[i * rows : (i + 1) * rows, state : 2 * state] = (
                totals[i] - high.astype(F32)
            ).astype(BF16)

    def finish(k, inside, side, own):
        from_k = slab[k, side : side + state, :]
        far = dot(sab[...], jnp.concatenate([from_k, from_k], axis=0))
        signs = (1.0, -1.0) if own == 1 else (-1.0, 1.0)
        out = spread(a_s, k) * (far[0:rows] + signs[0] * inside[0:rows])
        out = out + spread(b_s, k) * (far[rows : 2 * rows] + signs[1] * inside[rows : 2 * rows])
        value = x_s[k].astype(F32)
        skip = jnp.concatenate(
            [value[h * width : (h + 1) * width, :] * gain[h] for h in range(heads)], axis=0
        )
        return (out + skip).astype(BF16)

    def x_chunk(c, sums):
        to_space(feat.at[part(xor(nsp, me, c)), :], x_s.at[me], x_ss, x_rs, c).wait_recv()
        return take_chunk(xor(nsp, me, c), sums, w_t)

    sums = take_chunk(me, none, w_t)
    sums = lax.fori_loop(1, nsp // 2, x_chunk, sums)
    t_copies = {
        c: to_space(t_p.at[xor(nsp, me, c)], t_s.at[me], t_ss, t_rs, c) for c in range(1, nsp)
    }
    for c in reversed(range(1, nsp)):
        x_copies[c].wait_send()
        t_copies[c].start()
    t_s[me] = t_p[me]
    sums = lax.fori_loop(nsp // 2, nsp, x_chunk, sums)
    states = send_states(0, sums)
    take_states(0, states, 1)

    def mixed_copy(c):
        return to_space(mix_s.at[xor(nsp, me, c)], mixed_o.at[part(me), :], m_ss, m_rs, c)

    def forward(i, carry):
        c = nsp - 1 - i
        k = xor(nsp, me, c)
        mix_s[k] = finish(k, dot(xab[...], columns(k)), state, 1)

        @pl.when(c > 0)
        def _():
            mixed_copy(c).start()

        return carry

    lax.fori_loop(0, nsp, forward, 0)
    mixed_o[part(me), :] = mix_s[me]

    def residue(j, sums):
        keep = slab[j, 2 * state : 2 * state + 16, :].astype(F32)[0:1, :]
        wanted = lax.dot_general(
            t_s[j], picks(j), (((0,), (0,)), ((), ())), preferred_element_type=F32
        )
        x_s[j] = (keep * (mix_s[j].astype(F32) - wanted)).astype(BF16)
        return take_chunk(j, sums, q_t)

    def next_residue(c, sums):
        to_space(t_p.at[xor(nsp, me, c)], t_s.at[me], t_ss, t_rs, c).wait_recv()
        return residue(xor(nsp, me, c), sums)

    sums = lax.fori_loop(1, nsp, next_residue, residue(me, none))
    grad_states = send_states(1, sums)
    take_states(1, grad_states, 0)

    def grad_copy(c):
        return to_space(grad_s.at[xor(nsp, me, c)], grad_o.at[part(me), :], g_ss, g_rs, c)

    def backward(i, carry):
        c = nsp - 1 - i
        k = xor(nsp, me, c)
        grad_s[k] = finish(k, dot_nt(xab[...], lines(k)), 0, 0)

        @pl.when(c > 0)
        def _():
            grad_copy(c).start()

        return carry

    lax.fori_loop(0, nsp, backward, 0)
    grad_o[part(me), :] = grad_s[me]

    for c in range(1, nsp):
        key_copies[c].wait_send()
        t_copies[c].wait_send()
    for copies in (tot_copies, states, grad_states):
        for copy in copies:
            copy.wait_send()
    for c in range(1, nsp):
        mixed_copy(c).wait()
        grad_copy(c).wait()


def per_device(
    features, targets, write_keys, read_queries, decay_codes, scan_order, masked, skip_gain
):
    nsp, nsq = lax.axis_size("space"), lax.axis_size("seq")
    heads = decay_codes.shape[0]
    inner, tok = features.shape
    state = write_keys.shape[0]
    length = nsp * tok
    rows = inner // nsp
    unit = 0.065536 / (length * nsq)
    fits = length * length <= 8 * 1024 * 1024
    hp = 16 * (-(-heads // 16))
    vmem = pl.BlockSpec(memory_space=pltpu.VMEM)
    dma = pltpu.SemaphoreType.DMA
    return pl.pallas_call(
        partial(kernel, nsp, nsq, heads, unit),
        out_shape=(
            jax.ShapeDtypeStruct((inner, tok), BF16), jax.ShapeDtypeStruct((inner, tok), BF16)
        ),
        in_specs=[vmem] * 7 + [pl.BlockSpec(memory_space=pltpu.SMEM)],
        out_specs=(vmem, vmem),
        scratch_shapes=[
            pltpu.VMEM((nsp, rows, tok), BF16),
            pltpu.VMEM((nsp, masked.shape[0], rows), BF16),
            pltpu.VMEM((nsp, masked.shape[0], rows), BF16),
            pltpu.VMEM((nsp, 2 * state + 16, tok), BF16),
            pltpu.VMEM((2 * rows, length), BF16),
            pltpu.VMEM((nsp, rows, tok), BF16),
            pltpu.VMEM((nsp, rows, tok), BF16),
            pltpu.VMEM((length, length if fits else tok), BF16),
            pltpu.VMEM((16 if fits else tok, length), BF16),
            pltpu.VMEM((length, state), BF16),
            pltpu.VMEM((length, state), BF16),
            pltpu.VMEM((length, 128), F32),
            pltpu.VMEM((nsp, 8, tok), F32),
            pltpu.VMEM((hp, length), F32),
            pltpu.VMEM((nsp, hp, tok), F32),
            pltpu.VMEM((nsp, hp, tok), F32),
            pltpu.VMEM((hp, 128), F32),
            pltpu.VMEM((nsq, hp, 128), F32),
            pltpu.VMEM((2, 2, rows, state), F32),
            pltpu.VMEM((2, nsq, rows, state), F32),
            pltpu.VMEM((2 * rows, 2 * state), BF16),
            *[dma((nsp,)) for _ in range(10)],
            dma((nsq,)), dma((nsq,)),
            dma((2, nsq)), dma((2, nsq)),
        ],
        compiler_params=pltpu.CompilerParams(
            collective_id=0, has_side_effects=True, vmem_limit_bytes=56 * 1024 * 1024
        ),
    )(
        features, targets, write_keys, read_queries, decay_codes,
        scan_order.reshape(1, length), masked.reshape(1, masked.shape[0]), skip_gain,
    )


def solution(mesh):
    return jax.shard_map(
        per_device,
        mesh=mesh,
        in_specs=(
            P(None, ("seq", "space")),
            P(None, ("seq", "space")),
            P(None, ("seq", "space")),
            P(None, ("seq", "space")),
            P("space", "seq"),
            P(),
            P(("seq", "space")),
            P("space"),
        ),
        out_specs=(P(None, ("seq", "space")), P(None, ("seq", "space"))),
        check_vma=False,
    )
```

```python
from functools import partial

import jax
import jax.numpy as jnp
from jax import lax
from jax.experimental import pallas as pl
from jax.experimental.pallas import tpu as pltpu
from jax.sharding import PartitionSpec as P

MESH = pl.DeviceIdType.MESH
F32 = jnp.float32
BF16 = jnp.bfloat16


def dot(a, b):
    return jnp.dot(a, b, preferred_element_type=F32)


def dot_nt(a, b):
    return lax.dot_general(a, b, (((1,), (1,)), ((), ())), preferred_element_type=F32)


def xor(n, me, i):
    out, m = 0, 1
    while m < n:
        x, y = (me // m) % 2, (i // m) % 2
        out = out + m * (x + y - 2 * x * y)
        m *= 2
    return out


def kernel(
    nsp, nsq, heads, unit,
    feat, targ, write, read, codes, order, masked, gain,
    mixed_o, grad_o,
    x_s, t_s, t_p, slab, xab, mix_s, grad_s, gm_c, gm_r, w_t, q_t, rank_c, rank_r, codes_f, a_s, b_s,
    tot_s, tot_r, st_s, st_r, sab,
    key_ss, key_rs, x_ss, x_rs, t_ss, t_rs, m_ss, m_rs, g_ss, g_rs, tot_ss, tot_rs, st_ss, st_rs,
):
    me, mine = lax.axis_index("space"), lax.axis_index("seq")
    tok = feat.shape[1]
    rows = feat.shape[0] // nsp
    state = w_t.shape[1]
    width = rows // heads

    def chunk(i):
        return pl.ds(pl.multiple_of(i * tok, tok), tok)

    def part(i):
        return pl.ds(pl.multiple_of(i * rows, rows), rows)

    def to_space(src, dst, ss, rs, c):
        return pltpu.make_async_remote_copy(
            src_ref=src, dst_ref=dst, send_sem=ss.at[c], recv_sem=rs.at[c],
            device_id={"space": xor(nsp, me, c)}, device_id_type=MESH,
        )

    def to_seq(src, dst, ss, rs, c):
        return pltpu.make_async_remote_copy(
            src_ref=src, dst_ref=dst, send_sem=ss.at[c], recv_sem=rs.at[c],
            device_id={"seq": xor(nsq, mine, c)}, device_id_type=MESH,
        )

    barrier = pltpu.get_barrier_semaphore()
    for c in range(1, nsp):
        pl.semaphore_signal(barrier, inc=1, device_id={"space": xor(nsp, me, c)}, device_id_type=MESH)
    for c in range(1, nsq):
        pl.semaphore_signal(barrier, inc=1, device_id={"seq": xor(nsq, mine, c)}, device_id_type=MESH)
    slab[me, 0:state, :] = write[...]
    slab[me, state : 2 * state, :] = read[...]
    token = lax.broadcasted_iota(jnp.int32, (tok, masked.shape[1]), 0) + (mine * nsp + me) * tok
    hit = jnp.max(jnp.where(masked[...] == token, 1.0, 0.0), axis=1, keepdims=True)
    hit = jnp.transpose(jnp.broadcast_to(hit, (tok, 128)))[0:16, :]
    slab[me, 2 * state : 2 * state + 16, :] = hit.astype(BF16)
    codes_f[...] = jnp.zeros_like(codes_f)
    codes_f[0:heads, :] = codes[...].astype(F32)
    tot_s[...] = jnp.broadcast_to(jnp.sum(codes_f[...], axis=1, keepdims=True), tot_s.shape)
    pl.semaphore_wait(barrier, nsp + nsq - 2)

    def key_copy(m, c):
        place = xor(nsp, me, c)
        return pltpu.make_async_remote_copy(
            src_ref=slab.at[place], dst_ref=slab.at[place], send_sem=key_ss.at[m + c],
            recv_sem=key_rs.at[m + c], device_id={"space": xor(nsp, me, m)}, device_id_type=MESH,
        )

    key_copies = {}

    def key_step(m):
        held = range(0, nsp, 2 * m)
        for c in held:
            if c % (4 * m):
                key_copies[c].wait_recv()
        for c in held:
            key_copies[m + c] = key_copy(m, c)
            key_copies[m + c].start()

    key_step(nsp // 2)
    tot_copies = [to_seq(tot_s, tot_r.at[c], tot_ss, tot_rs, c) for c in range(1, nsq)]
    for copy in tot_copies:
        copy.start()
    x_copies = {
        c: to_space(feat.at[part(xor(nsp, me, c)), :], x_s.at[me], x_ss, x_rs, c) for c in range(1, nsp)
    }
    for c in range(1, nsp // 2):
        x_copies[c].start()
    x_s[me] = feat[part(me), :]

    length = nsp * tok
    places = lax.broadcasted_iota(jnp.int32, (tok, length), 1).astype(F32)

    def rank_chunk(i, carry):
        token = lax.broadcasted_iota(jnp.int32, (tok, length), 0) + i * tok
        rank = jnp.sum(jnp.where(order[...] == token, places, 0.0), axis=1, keepdims=True)
        wide = jnp.broadcast_to(rank, (tok, 128))
        rank_c[chunk(i), :] = wide
        rank_r[i] = jnp.transpose(wide)[0:8, :]
        return carry

    lax.fori_loop(0, nsp, rank_chunk, 0)

    def picks(j):
        keep = slab[j, 2 * state : 2 * state + 16, :]
        older = lax.broadcasted_iota(jnp.int32, (tok, tok), 0) <= lax.broadcasted_iota(
            jnp.int32, (tok, tok), 1
        )
        count = dot(keep, jnp.where(older, 1.0, 0.0).astype(BF16))[0:1, :]
        slot = lax.broadcasted_iota(jnp.int32, (masked.shape[1], tok), 0).astype(F32) + 1.0
        return jnp.where(count == slot, keep.astype(F32)[0:1, :], 0.0).astype(BF16)

    def before(j, k):
        col = rank_c[chunk(j), :]
        return jnp.concatenate([col] * (tok // 128), axis=1) <= rank_r[k][0:1, :]

    m = nsp // 4
    key_step(m)
    for c in reversed(range(nsp // 2, nsp)):
        x_copies[c].start()

    def pack(d, carry):
        t_p[d] = dot_nt(picks(me), targ[part(d), :]).astype(BF16)
        return carry

    lax.fori_loop(0, nsp, pack, 0)

    for copy in tot_copies:
        copy.wait_recv()
    offset = jnp.zeros(tot_s.shape, F32)
    for c in range(1, nsq):
        offset = offset + jnp.where(xor(nsq, mine, c) < mine, tot_r[c], 0.0)

    def run_chunk(k, carry):
        def add(j, acc):
            return acc + dot(
                codes_f[:, chunk(j)].astype(BF16), jnp.where(before(j, k), 1.0, 0.0).astype(BF16)
            )

        run = lax.fori_loop(0, nsp, add, jnp.broadcast_to(offset[:, 0:1], (codes_f.shape[0], tok)))
        a_s[k] = jnp.exp(-unit * run)
        b_s[k] = jnp.exp(unit * run)
        return carry

    lax.fori_loop(0, nsp, run_chunk, 0)

    while m > 1:
        m //= 2
        key_step(m)
    t_copies = {
        c: to_space(t_p.at[xor(nsp, me, c)], t_s.at[me], t_ss, t_rs, c) for c in range(1, nsp)
    }
    for c in reversed(range(1, nsp)):
        x_copies[c].wait_send()
        t_copies[c].start()
    t_s[me] = t_p[me]
    for c in range(1, nsp, 2):
        key_copies[c].wait_recv()

    def flip(i, carry):
        w_t[chunk(i), :] = jnp.transpose(slab[i, 0:state, :].astype(F32)).astype(BF16)
        q_t[chunk(i), :] = jnp.transpose(slab[i, state : 2 * state, :].astype(F32)).astype(BF16)
        return carry

    lax.fori_loop(0, nsp, flip, 0)

    def spread(ref, k):
        t = ref[k]
        return jnp.concatenate(
            [jnp.broadcast_to(t[h : h + 1, :], (width, tok)) for h in range(heads)], axis=0
        )

    def gram(j, k):
        tile = dot(w_t[chunk(j), :], slab[k, state : 2 * state, :])
        return jnp.where(before(j, k), tile, 0.0).astype(BF16)

    whole = gm_c.shape[1] == length

    def columns(k):
        if whole:
            return gm_c[:, chunk(k)]

        def fill(j, carry):
            gm_c[chunk(j), :] = gram(j, k)
            return carry

        lax.fori_loop(0, nsp, fill, 0)
        return gm_c[...]

    def lines(j):
        if whole:
            return gm_c[chunk(j), :]

        def fill(k, carry):
            gm_r[:, chunk(k)] = gram(j, k)
            return carry

        lax.fori_loop(0, nsp, fill, 0)
        return gm_r[...]

    def take_chunk(j, sums, into_t):
        value = x_s[j].astype(F32)
        wide = jnp.concatenate([value * spread(b_s, j), value * spread(a_s, j)], axis=0)
        high = wide.astype(BF16)
        low = (wide - high.astype(F32)).astype(BF16)
        xab[:, chunk(j)] = high
        into = into_t[chunk(j), :]
        return sums + (dot(high, into) + dot(low, into))

    none = jnp.zeros((2 * rows, state), F32)

    def send_states(turn, sums):
        st_s[turn, 0] = sums[0:rows]
        st_s[turn, 1] = sums[rows : 2 * rows]
        copies = []
        for c in range(1, nsq):
            there = xor(nsq, mine, c)
            which = (nsq + mine - there) // nsq
            copies.append(
                to_seq(
                    st_s.at[turn, which], st_r.at[turn, c], st_ss.at[turn], st_rs.at[turn], c
                )
            )
            copies[-1].start()
        return copies

    def take_states(turn, copies, own):
        totals = [jnp.zeros((rows, state), F32), jnp.zeros((rows, state), F32)]
        totals[own] = st_s[turn, own]
        for c in range(1, nsq):
            copies[c - 1].wait_recv()
            got = st_r[turn, c]
            there = xor(nsq, mine, c)
            totals[0] = totals[0] + jnp.where(there < mine, got, 0.0)
            totals[1] = totals[1] + jnp.where(there > mine, got, 0.0)
        for i in range(2):
            high = totals[i].astype(BF16)
            sab[i * rows : (i + 1) * rows, 0:state] = high
            sab[i * rows : (i + 1) * rows, state : 2 * state] = (
                totals[i] - high.astype(F32)
            ).astype(BF16)

    def finish(k, inside, side, own):
        from_k = slab[k, side : side + state, :]
        far = dot(sab[...], jnp.concatenate([from_k, from_k], axis=0))
        signs = (1.0, -1.0) if own == 1 else (-1.0, 1.0)
        out = spread(a_s, k) * (far[0:rows] + signs[0] * inside[0:rows])
        out = out + spread(b_s, k) * (far[rows : 2 * rows] + signs[1] * inside[rows : 2 * rows])
        value = x_s[k].astype(F32)
        skip = jnp.concatenate(
            [value[h * width : (h + 1) * width, :] * gain[h] for h in range(heads)], axis=0
        )
        return (out + skip).astype(BF16)

    def x_chunk(c, sums):
        to_space(feat.at[part(xor(nsp, me, c)), :], x_s.at[me], x_ss, x_rs, c).wait_recv()
        return take_chunk(xor(nsp, me, c), sums, w_t)

    sums = take_chunk(me, none, w_t)
    sums = lax.fori_loop(1, nsp, x_chunk, sums)
    states = send_states(0, sums)
    if whole:

        def fill_all(j, carry):
            def fill(k, carry):
                gm_c[chunk(j), chunk(k)] = gram(j, k)
                return carry

            return lax.fori_loop(0, nsp, fill, carry)

        lax.fori_loop(0, nsp, fill_all, 0)

    take_states(0, states, 1)

    def mixed_copy(c):
        return to_space(mix_s.at[xor(nsp, me, c)], mixed_o.at[part(me), :], m_ss, m_rs, c)

    def forward(i, carry):
        c = nsp - 1 - i
        k = xor(nsp, me, c)
        mix_s[k] = finish(k, dot(xab[...], columns(k)), state, 1)

        @pl.when(c > 0)
        def _():
            mixed_copy(c).start()

        return carry

    lax.fori_loop(0, nsp, forward, 0)
    mixed_o[part(me), :] = mix_s[me]

    def residue(j, sums):
        keep = slab[j, 2 * state : 2 * state + 16, :].astype(F32)[0:1, :]
        wanted = lax.dot_general(
            t_s[j], picks(j), (((0,), (0,)), ((), ())), preferred_element_type=F32
        )
        x_s[j] = (keep * (mix_s[j].astype(F32) - wanted)).astype(BF16)
        return take_chunk(j, sums, q_t)

    def next_residue(c, sums):
        to_space(t_p.at[xor(nsp, me, c)], t_s.at[me], t_ss, t_rs, c).wait_recv()
        return residue(xor(nsp, me, c), sums)

    sums = lax.fori_loop(1, nsp, next_residue, residue(me, none))
    grad_states = send_states(1, sums)
    take_states(1, grad_states, 0)

    def grad_copy(c):
        return to_space(grad_s.at[xor(nsp, me, c)], grad_o.at[part(me), :], g_ss, g_rs, c)

    def backward(i, carry):
        c = nsp - 1 - i
        k = xor(nsp, me, c)
        grad_s[k] = finish(k, dot_nt(xab[...], lines(k)), 0, 0)

        @pl.when(c > 0)
        def _():
            grad_copy(c).start()

        return carry

    lax.fori_loop(0, nsp, backward, 0)
    grad_o[part(me), :] = grad_s[me]

    for c in range(1, nsp):
        key_copies[c].wait_send()
        t_copies[c].wait_send()
    for copies in (tot_copies, states, grad_states):
        for copy in copies:
            copy.wait_send()
    for c in range(1, nsp):
        mixed_copy(c).wait()
        grad_copy(c).wait()


def per_device(
    features, targets, write_keys, read_queries, decay_codes, scan_order, masked, skip_gain
):
    nsp, nsq = lax.axis_size("space"), lax.axis_size("seq")
    heads = decay_codes.shape[0]
    inner, tok = features.shape
    state = write_keys.shape[0]
    length = nsp * tok
    rows = inner // nsp
    unit = 0.065536 / (length * nsq)
    fits = length * length <= 8 * 1024 * 1024
    hp = 16 * (-(-heads // 16))
    vmem = pl.BlockSpec(memory_space=pltpu.VMEM)
    dma = pltpu.SemaphoreType.DMA
    return pl.pallas_call(
        partial(kernel, nsp, nsq, heads, unit),
        out_shape=(
            jax.ShapeDtypeStruct((inner, tok), BF16), jax.ShapeDtypeStruct((inner, tok), BF16)
        ),
        in_specs=[vmem] * 7 + [pl.BlockSpec(memory_space=pltpu.SMEM)],
        out_specs=(vmem, vmem),
        scratch_shapes=[
            pltpu.VMEM((nsp, rows, tok), BF16),
            pltpu.VMEM((nsp, masked.shape[0], rows), BF16),
            pltpu.VMEM((nsp, masked.shape[0], rows), BF16),
            pltpu.VMEM((nsp, 2 * state + 16, tok), BF16),
            pltpu.VMEM((2 * rows, length), BF16),
            pltpu.VMEM((nsp, rows, tok), BF16),
            pltpu.VMEM((nsp, rows, tok), BF16),
            pltpu.VMEM((length, length if fits else tok), BF16),
            pltpu.VMEM((16 if fits else tok, length), BF16),
            pltpu.VMEM((length, state), BF16),
            pltpu.VMEM((length, state), BF16),
            pltpu.VMEM((length, 128), F32),
            pltpu.VMEM((nsp, 8, tok), F32),
            pltpu.VMEM((hp, length), F32),
            pltpu.VMEM((nsp, hp, tok), F32),
            pltpu.VMEM((nsp, hp, tok), F32),
            pltpu.VMEM((hp, 128), F32),
            pltpu.VMEM((nsq, hp, 128), F32),
            pltpu.VMEM((2, 2, rows, state), F32),
            pltpu.VMEM((2, nsq, rows, state), F32),
            pltpu.VMEM((2 * rows, 2 * state), BF16),
            *[dma((nsp,)) for _ in range(10)],
            dma((nsq,)), dma((nsq,)),
            dma((2, nsq)), dma((2, nsq)),
        ],
        compiler_params=pltpu.CompilerParams(
            collective_id=0, has_side_effects=True, vmem_limit_bytes=56 * 1024 * 1024
        ),
    )(
        features, targets, write_keys, read_queries, decay_codes,
        scan_order.reshape(1, length), masked.reshape(1, masked.shape[0]), skip_gain,
    )


def solution(mesh):
    return jax.shard_map(
        per_device,
        mesh=mesh,
        in_specs=(
            P(None, ("seq", "space")),
            P(None, ("seq", "space")),
            P(None, ("seq", "space")),
            P(None, ("seq", "space")),
            P("space", "seq"),
            P(),
            P(("seq", "space")),
            P("space"),
        ),
        out_specs=(P(None, ("seq", "space")), P(None, ("seq", "space"))),
        check_vma=False,
    )
```

```python
from functools import partial

import jax
import jax.numpy as jnp
from jax import lax
from jax.experimental import pallas as pl
from jax.experimental.pallas import tpu as pltpu
from jax.sharding import PartitionSpec as P

MESH = pl.DeviceIdType.MESH
F32 = jnp.float32
BF16 = jnp.bfloat16


def dot(a, b):
    return jnp.dot(a, b, preferred_element_type=F32)


def dot_nt(a, b):
    return lax.dot_general(a, b, (((1,), (1,)), ((), ())), preferred_element_type=F32)


def xor(n, me, i):
    out, m = 0, 1
    while m < n:
        x, y = (me // m) % 2, (i // m) % 2
        out = out + m * (x + y - 2 * x * y)
        m *= 2
    return out


def kernel(
    nsp, nsq, heads, unit,
    feat, targ, write, read, codes, order, masked, gain,
    mixed_o, grad_o,
    x_s, t_s, t_p, slab, xab, mix_s, grad_s, gm_c, gm_r, w_t, q_t, rank_c, rank_r, codes_f, a_s, b_s,
    tot_s, tot_r, st_s, st_r, sab,
    key_ss, key_rs, x_ss, x_rs, t_ss, t_rs, m_ss, m_rs, g_ss, g_rs, tot_ss, tot_rs, st_ss, st_rs, own_ss, targ_s,
):
    me, mine = lax.axis_index("space"), lax.axis_index("seq")
    tok = feat.shape[1]
    rows = feat.shape[0] // nsp
    state = w_t.shape[1]
    width = rows // heads

    def chunk(i):
        return pl.ds(pl.multiple_of(i * tok, tok), tok)

    def part(i):
        return pl.ds(pl.multiple_of(i * rows, rows), rows)

    def to_space(src, dst, ss, rs, c):
        return pltpu.make_async_remote_copy(
            src_ref=src, dst_ref=dst, send_sem=ss.at[c], recv_sem=rs.at[c],
            device_id={"space": xor(nsp, me, c)}, device_id_type=MESH,
        )

    def to_seq(src, dst, ss, rs, c):
        return pltpu.make_async_remote_copy(
            src_ref=src, dst_ref=dst, send_sem=ss.at[c], recv_sem=rs.at[c],
            device_id={"seq": xor(nsq, mine, c)}, device_id_type=MESH,
        )

    barrier = pltpu.get_barrier_semaphore()
    for c in range(1, nsp):
        pl.semaphore_signal(barrier, inc=1, device_id={"space": xor(nsp, me, c)}, device_id_type=MESH)
    for c in range(1, nsq):
        pl.semaphore_signal(barrier, inc=1, device_id={"seq": xor(nsq, mine, c)}, device_id_type=MESH)
    slab[me, 0:state, :] = write[...]
    slab[me, state : 2 * state, :] = read[...]
    token = lax.broadcasted_iota(jnp.int32, (tok, masked.shape[1]), 0) + (mine * nsp + me) * tok
    hit = jnp.max(jnp.where(masked[...] == token, 1.0, 0.0), axis=1, keepdims=True)
    hit = jnp.transpose(jnp.broadcast_to(hit, (tok, 128)))[0:16, :]
    slab[me, 2 * state : 2 * state + 16, :] = hit.astype(BF16)
    codes_f[...] = jnp.zeros_like(codes_f)
    codes_f[0:heads, :] = codes[...].astype(F32)
    tot_s[...] = jnp.broadcast_to(jnp.sum(codes_f[...], axis=1, keepdims=True), tot_s.shape)
    pl.semaphore_wait(barrier, nsp + nsq - 2)

    def key_copy(m, c):
        place = xor(nsp, me, c)
        return pltpu.make_async_remote_copy(
            src_ref=slab.at[place], dst_ref=slab.at[place], send_sem=key_ss.at[m + c],
            recv_sem=key_rs.at[m + c], device_id={"space": xor(nsp, me, m)}, device_id_type=MESH,
        )

    key_copies = {}

    def key_step(m):
        held = range(0, nsp, 2 * m)
        for c in held:
            if c % (4 * m):
                key_copies[c].wait_recv()
        for c in held:
            key_copies[m + c] = key_copy(m, c)
            key_copies[m + c].start()

    own_t = pltpu.make_async_copy(targ, targ_s, own_ss.at[1])
    own_t.start()
    key_step(nsp // 2)
    tot_copies = [to_seq(tot_s, tot_r.at[c], tot_ss, tot_rs, c) for c in range(1, nsq)]
    for copy in tot_copies:
        copy.start()
    x_copies = {
        c: to_space(feat.at[part(xor(nsp, me, c)), :], x_s.at[me], x_ss, x_rs, c) for c in range(1, nsp)
    }
    for c in range(1, nsp // 2):
        x_copies[c].start()
    own_x = pltpu.make_async_copy(feat.at[part(me), :], x_s.at[me], own_ss.at[0])
    own_x.start()

    length = nsp * tok
    places = lax.broadcasted_iota(jnp.int32, (tok, length), 1).astype(F32)

    def rank_chunk(i, carry):
        token = lax.broadcasted_iota(jnp.int32, (tok, length), 0) + i * tok
        rank = jnp.sum(jnp.where(order[...] == token, places, 0.0), axis=1, keepdims=True)
        wide = jnp.broadcast_to(rank, (tok, 128))
        rank_c[chunk(i), :] = wide
        rank_r[i] = jnp.transpose(wide)[0:8, :]
        return carry

    lax.fori_loop(0, nsp, rank_chunk, 0)

    def picks(j):
        keep = slab[j, 2 * state : 2 * state + 16, :]
        older = lax.broadcasted_iota(jnp.int32, (tok, tok), 0) <= lax.broadcasted_iota(
            jnp.int32, (tok, tok), 1
        )
        count = dot(keep, jnp.where(older, 1.0, 0.0).astype(BF16))[0:1, :]
        slot = lax.broadcasted_iota(jnp.int32, (masked.shape[1], tok), 0).astype(F32) + 1.0
        return jnp.where(count == slot, keep.astype(F32)[0:1, :], 0.0).astype(BF16)

    def before(j, k):
        col = rank_c[chunk(j), :]
        return jnp.concatenate([col] * (tok // 128), axis=1) <= rank_r[k][0:1, :]

    m = nsp // 4
    key_step(m)
    for c in reversed(range(nsp // 2, nsp)):
        x_copies[c].start()

    own_t.wait()

    def pack(d, carry):
        t_p[d] = dot_nt(picks(me), targ_s[part(d), :]).astype(BF16)
        return carry

    lax.fori_loop(0, nsp, pack, 0)
    while m > 1:
        m //= 2
        key_step(m)

    for copy in tot_copies:
        copy.wait_recv()
    offset = jnp.zeros(tot_s.shape, F32)
    for c in range(1, nsq):
        offset = offset + jnp.where(xor(nsq, mine, c) < mine, tot_r[c], 0.0)

    def run_chunk(k, carry):
        def add(j, acc):
            return acc + dot(
                codes_f[:, chunk(j)].astype(BF16), jnp.where(before(j, k), 1.0, 0.0).astype(BF16)
            )

        run = lax.fori_loop(0, nsp, add, jnp.broadcast_to(offset[:, 0:1], (codes_f.shape[0], tok)))
        a_s[k] = jnp.exp(-unit * run)
        b_s[k] = jnp.exp(unit * run)
        return carry

    lax.fori_loop(0, nsp, run_chunk, 0)

    t_copies = {
        c: to_space(t_p.at[xor(nsp, me, c)], t_s.at[me], t_ss, t_rs, c) for c in range(1, nsp)
    }
    for c in reversed(range(1, nsp)):
        x_copies[c].wait_send()
        t_copies[c].start()
    t_s[me] = t_p[me]
    for c in range(1, nsp, 2):
        key_copies[c].wait_recv()

    def flip(i, carry):
        w_t[chunk(i), :] = jnp.transpose(slab[i, 0:state, :].astype(F32)).astype(BF16)
        q_t[chunk(i), :] = jnp.transpose(slab[i, state : 2 * state, :].astype(F32)).astype(BF16)
        return carry

    lax.fori_loop(0, nsp, flip, 0)

    def spread(ref, k):
        t = ref[k]
        return jnp.concatenate(
            [jnp.broadcast_to(t[h : h + 1, :], (width, tok)) for h in range(heads)], axis=0
        )

    def gram(j, k):
        tile = dot(w_t[chunk(j), :], slab[k, state : 2 * state, :])
        return jnp.where(before(j, k), tile, 0.0).astype(BF16)

    whole = gm_c.shape[1] == length

    def columns(k):
        if whole:
            return gm_c[:, chunk(k)]

        def fill(j, carry):
            gm_c[chunk(j), :] = gram(j, k)
            return carry

        lax.fori_loop(0, nsp, fill, 0)
        return gm_c[...]

    def lines(j):
        if whole:
            return gm_c[chunk(j), :]

        def fill(k, carry):
            gm_r[:, chunk(k)] = gram(j, k)
            return carry

        lax.fori_loop(0, nsp, fill, 0)
        return gm_r[...]

    def take_chunk(j, sums, into_t):
        value = x_s[j].astype(F32)
        wide = jnp.concatenate([value * spread(b_s, j), value * spread(a_s, j)], axis=0)
        high = wide.astype(BF16)
        low = (wide - high.astype(F32)).astype(BF16)
        xab[:, chunk(j)] = high
        into = into_t[chunk(j), :]
        return sums + (dot(high, into) + dot(low, into))

    none = jnp.zeros((2 * rows, state), F32)

    def send_states(turn, sums):
        st_s[turn, 0] = sums[0:rows]
        st_s[turn, 1] = sums[rows : 2 * rows]
        copies = []
        for c in range(1, nsq):
            there = xor(nsq, mine, c)
            which = (nsq + mine - there) // nsq
            copies.append(
                to_seq(
                    st_s.at[turn, which], st_r.at[turn, c], st_ss.at[turn], st_rs.at[turn], c
                )
            )
            copies[-1].start()
        return copies

    def take_states(turn, copies, own):
        totals = [jnp.zeros((rows, state), F32), jnp.zeros((rows, state), F32)]
        totals[own] = st_s[turn, own]
        for c in range(1, nsq):
            copies[c - 1].wait_recv()
            got = st_r[turn, c]
            there = xor(nsq, mine, c)
            totals[0] = totals[0] + jnp.where(there < mine, got, 0.0)
            totals[1] = totals[1] + jnp.where(there > mine, got, 0.0)
        for i in range(2):
            high = totals[i].astype(BF16)
            sab[i * rows : (i + 1) * rows, 0:state] = high
            sab[i * rows : (i + 1) * rows, state : 2 * state] = (
                totals[i] - high.astype(F32)
            ).astype(BF16)

    def finish(k, inside, side, own):
        from_k = slab[k, side : side + state, :]
        far = dot(sab[...], jnp.concatenate([from_k, from_k], axis=0))
        signs = (1.0, -1.0) if own == 1 else (-1.0, 1.0)
        out = spread(a_s, k) * (far[0:rows] + signs[0] * inside[0:rows])
        out = out + spread(b_s, k) * (far[rows : 2 * rows] + signs[1] * inside[rows : 2 * rows])
        value = x_s[k].astype(F32)
        skip = jnp.concatenate(
            [value[h * width : (h + 1) * width, :] * gain[h] for h in range(heads)], axis=0
        )
        return (out + skip).astype(BF16)

    def x_chunk(c, sums):
        to_space(feat.at[part(xor(nsp, me, c)), :], x_s.at[me], x_ss, x_rs, c).wait_recv()
        return take_chunk(xor(nsp, me, c), sums, w_t)

    own_x.wait()
    sums = take_chunk(me, none, w_t)
    sums = lax.fori_loop(1, nsp, x_chunk, sums)
    states = send_states(0, sums)
    if whole:

        def fill_all(j, carry):
            def fill(k, carry):
                gm_c[chunk(j), chunk(k)] = gram(j, k)
                return carry

            return lax.fori_loop(0, nsp, fill, carry)

        lax.fori_loop(0, nsp, fill_all, 0)

    take_states(0, states, 1)

    def mixed_copy(c):
        return to_space(mix_s.at[xor(nsp, me, c)], mixed_o.at[part(me), :], m_ss, m_rs, c)

    def forward(i, carry):
        c = nsp - 1 - i
        k = xor(nsp, me, c)
        mix_s[k] = finish(k, dot(xab[...], columns(k)), state, 1)

        @pl.when(c > 0)
        def _():
            mixed_copy(c).start()

        return carry

    lax.fori_loop(0, nsp, forward, 0)
    own_m = pltpu.make_async_copy(mix_s.at[me], mixed_o.at[part(me), :], own_ss.at[2])
    own_m.start()

    def residue(j, sums):
        keep = slab[j, 2 * state : 2 * state + 16, :].astype(F32)[0:1, :]
        wanted = lax.dot_general(
            t_s[j], picks(j), (((0,), (0,)), ((), ())), preferred_element_type=F32
        )
        x_s[j] = (keep * (mix_s[j].astype(F32) - wanted)).astype(BF16)
        return take_chunk(j, sums, q_t)

    def next_residue(c, sums):
        to_space(t_p.at[xor(nsp, me, c)], t_s.at[me], t_ss, t_rs, c).wait_recv()
        return residue(xor(nsp, me, c), sums)

    sums = lax.fori_loop(1, nsp, next_residue, residue(me, none))
    grad_states = send_states(1, sums)
    take_states(1, grad_states, 0)

    def grad_copy(c):
        return to_space(grad_s.at[xor(nsp, me, c)], grad_o.at[part(me), :], g_ss, g_rs, c)

    def backward(i, carry):
        c = nsp - 1 - i
        k = xor(nsp, me, c)
        grad_s[k] = finish(k, dot_nt(xab[...], lines(k)), 0, 0)

        @pl.when(c > 0)
        def _():
            grad_copy(c).start()

        return carry

    lax.fori_loop(0, nsp, backward, 0)
    own_g = pltpu.make_async_copy(grad_s.at[me], grad_o.at[part(me), :], own_ss.at[3])
    own_g.start()

    for c in range(1, nsp):
        key_copies[c].wait_send()
        t_copies[c].wait_send()
    for copies in (tot_copies, states, grad_states):
        for copy in copies:
            copy.wait_send()
    for c in range(1, nsp):
        mixed_copy(c).wait()
        grad_copy(c).wait()
    own_m.wait()
    own_g.wait()


def per_device(
    features, targets, write_keys, read_queries, decay_codes, scan_order, masked, skip_gain
):
    nsp, nsq = lax.axis_size("space"), lax.axis_size("seq")
    heads = decay_codes.shape[0]
    inner, tok = features.shape
    state = write_keys.shape[0]
    length = nsp * tok
    rows = inner // nsp
    unit = 0.065536 / (length * nsq)
    fits = length * length <= 8 * 1024 * 1024
    hp = 16 * (-(-heads // 16))
    vmem = pl.BlockSpec(memory_space=pltpu.VMEM)
    hbm = pl.BlockSpec(memory_space=pl.ANY)
    dma = pltpu.SemaphoreType.DMA
    return pl.pallas_call(
        partial(kernel, nsp, nsq, heads, unit),
        out_shape=(
            jax.ShapeDtypeStruct((inner, tok), BF16), jax.ShapeDtypeStruct((inner, tok), BF16)
        ),
        in_specs=[hbm] * 2 + [vmem] * 5 + [pl.BlockSpec(memory_space=pltpu.SMEM)],
        out_specs=(hbm, hbm),
        scratch_shapes=[
            pltpu.VMEM((nsp, rows, tok), BF16),
            pltpu.VMEM((nsp, masked.shape[0], rows), BF16),
            pltpu.VMEM((nsp, masked.shape[0], rows), BF16),
            pltpu.VMEM((nsp, 2 * state + 16, tok), BF16),
            pltpu.VMEM((2 * rows, length), BF16),
            pltpu.VMEM((nsp, rows, tok), BF16),
            pltpu.VMEM((nsp, rows, tok), BF16),
            pltpu.VMEM((length, length if fits else tok), BF16),
            pltpu.VMEM((16 if fits else tok, length), BF16),
            pltpu.VMEM((length, state), BF16),
            pltpu.VMEM((length, state), BF16),
            pltpu.VMEM((length, 128), F32),
            pltpu.VMEM((nsp, 8, tok), F32),
            pltpu.VMEM((hp, length), F32),
            pltpu.VMEM((nsp, hp, tok), F32),
            pltpu.VMEM((nsp, hp, tok), F32),
            pltpu.VMEM((hp, 128), F32),
            pltpu.VMEM((nsq, hp, 128), F32),
            pltpu.VMEM((2, 2, rows, state), F32),
            pltpu.VMEM((2, nsq, rows, state), F32),
            pltpu.VMEM((2 * rows, 2 * state), BF16),
            *[dma((nsp,)) for _ in range(10)],
            dma((nsq,)), dma((nsq,)),
            dma((2, nsq)), dma((2, nsq)), dma((4,)),
            pltpu.VMEM((inner, tok), BF16),
        ],
        compiler_params=pltpu.CompilerParams(
            collective_id=0, has_side_effects=True, vmem_limit_bytes=56 * 1024 * 1024
        ),
    )(
        features, targets, write_keys, read_queries, decay_codes,
        scan_order.reshape(1, length), masked.reshape(1, masked.shape[0]), skip_gain,
    )


def solution(mesh):
    return jax.shard_map(
        per_device,
        mesh=mesh,
        in_specs=(
            P(None, ("seq", "space")),
            P(None, ("seq", "space")),
            P(None, ("seq", "space")),
            P(None, ("seq", "space")),
            P("space", "seq"),
            P(),
            P(("seq", "space")),
            P("space"),
        ),
        out_specs=(P(None, ("seq", "space")), P(None, ("seq", "space"))),
        check_vma=False,
    )
```

```python
from functools import partial

import jax
import jax.numpy as jnp
from jax import lax
from jax.experimental import pallas as pl
from jax.experimental.pallas import tpu as pltpu
from jax.sharding import PartitionSpec as P

MESH = pl.DeviceIdType.MESH
F32 = jnp.float32
BF16 = jnp.bfloat16


def dot(a, b):
    return jnp.dot(a, b, preferred_element_type=F32)


def dot_nt(a, b):
    return lax.dot_general(a, b, (((1,), (1,)), ((), ())), preferred_element_type=F32)


def xor(n, me, i):
    out, m = 0, 1
    while m < n:
        x, y = (me // m) % 2, (i // m) % 2
        out = out + m * (x + y - 2 * x * y)
        m *= 2
    return out


def kernel(
    nsp, nsq, heads, unit,
    feat, targ, write, read, codes, order, masked, gain,
    mixed_o, grad_o,
    x_s, t_s, t_p, slab, xab, mix_s, grad_s, gm_c, gm_r, w_t, q_t, rank_c, rank_r, codes_f, a_s, b_s,
    tot_s, tot_r, st_s, st_r, sab,
    key_ss, key_rs, x_ss, x_rs, t_ss, t_rs, m_ss, m_rs, g_ss, g_rs, tot_ss, tot_rs, st_ss, st_rs, own_ss, targ_s,
):
    me, mine = lax.axis_index("space"), lax.axis_index("seq")
    tok = feat.shape[1]
    rows = feat.shape[0] // nsp
    state = w_t.shape[1]
    width = rows // heads

    def chunk(i):
        return pl.ds(pl.multiple_of(i * tok, tok), tok)

    def part(i):
        return pl.ds(pl.multiple_of(i * rows, rows), rows)

    def to_space(src, dst, ss, rs, c):
        return pltpu.make_async_remote_copy(
            src_ref=src, dst_ref=dst, send_sem=ss.at[c], recv_sem=rs.at[c],
            device_id={"space": xor(nsp, me, c)}, device_id_type=MESH,
        )

    def to_seq(src, dst, ss, rs, c):
        return pltpu.make_async_remote_copy(
            src_ref=src, dst_ref=dst, send_sem=ss.at[c], recv_sem=rs.at[c],
            device_id={"seq": xor(nsq, mine, c)}, device_id_type=MESH,
        )

    barrier = pltpu.get_barrier_semaphore()
    for c in range(1, nsp):
        pl.semaphore_signal(barrier, inc=1, device_id={"space": xor(nsp, me, c)}, device_id_type=MESH)
    for c in range(1, nsq):
        pl.semaphore_signal(barrier, inc=1, device_id={"seq": xor(nsq, mine, c)}, device_id_type=MESH)
    slab[me, 0:state, :] = write[...]
    slab[me, state : 2 * state, :] = read[...]
    token = lax.broadcasted_iota(jnp.int32, (tok, masked.shape[1]), 0) + (mine * nsp + me) * tok
    hit = jnp.max(jnp.where(masked[...] == token, 1.0, 0.0), axis=1, keepdims=True)
    hit = jnp.transpose(jnp.broadcast_to(hit, (tok, 128)))[0:16, :]
    slab[me, 2 * state : 2 * state + 16, :] = hit.astype(BF16)
    codes_f[...] = jnp.zeros_like(codes_f)
    codes_f[0:heads, :] = codes[...].astype(F32)
    tot_s[...] = jnp.broadcast_to(jnp.sum(codes_f[...], axis=1, keepdims=True), tot_s.shape)
    pl.semaphore_wait(barrier, nsp + nsq - 2)

    def key_copy(m, c):
        place = xor(nsp, me, c)
        return pltpu.make_async_remote_copy(
            src_ref=slab.at[place], dst_ref=slab.at[place], send_sem=key_ss.at[m + c],
            recv_sem=key_rs.at[m + c], device_id={"space": xor(nsp, me, m)}, device_id_type=MESH,
        )

    key_copies = {}

    def key_step(m):
        held = range(0, nsp, 2 * m)
        for c in held:
            if c % (4 * m):
                key_copies[c].wait_recv()
        for c in held:
            key_copies[m + c] = key_copy(m, c)
            key_copies[m + c].start()

    own_t = pltpu.make_async_copy(targ, targ_s, own_ss.at[1])
    own_t.start()
    key_step(nsp // 2)
    tot_copies = [to_seq(tot_s, tot_r.at[c], tot_ss, tot_rs, c) for c in range(1, nsq)]
    for copy in tot_copies:
        copy.start()
    x_copies = {
        c: to_space(feat.at[part(xor(nsp, me, c)), :], x_s.at[me], x_ss, x_rs, c) for c in range(1, nsp)
    }
    for c in (nsp - 1, *range(1, nsp // 2)):
        x_copies[c].start()
    own_x = pltpu.make_async_copy(feat.at[part(me), :], x_s.at[me], own_ss.at[0])
    own_x.start()

    length = nsp * tok
    places = lax.broadcasted_iota(jnp.int32, (tok, length), 1).astype(F32)

    def rank_chunk(i, carry):
        token = lax.broadcasted_iota(jnp.int32, (tok, length), 0) + i * tok
        rank = jnp.sum(jnp.where(order[...] == token, places, 0.0), axis=1, keepdims=True)
        wide = jnp.broadcast_to(rank, (tok, 128))
        rank_c[chunk(i), :] = wide
        rank_r[i] = jnp.transpose(wide)[0:8, :]
        return carry

    lax.fori_loop(0, nsp, rank_chunk, 0)

    def picks(j):
        keep = slab[j, 2 * state : 2 * state + 16, :]
        older = lax.broadcasted_iota(jnp.int32, (tok, tok), 0) <= lax.broadcasted_iota(
            jnp.int32, (tok, tok), 1
        )
        count = dot(keep, jnp.where(older, 1.0, 0.0).astype(BF16))[0:1, :]
        slot = lax.broadcasted_iota(jnp.int32, (masked.shape[1], tok), 0).astype(F32) + 1.0
        return jnp.where(count == slot, keep.astype(F32)[0:1, :], 0.0).astype(BF16)

    def before(j, k):
        col = rank_c[chunk(j), :]
        return jnp.concatenate([col] * (tok // 128), axis=1) <= rank_r[k][0:1, :]

    m = nsp // 4
    key_step(m)
    for c in reversed(range(nsp // 2, nsp - 1)):
        x_copies[c].start()

    own_t.wait()

    def pack(d, carry):
        t_p[d] = dot_nt(picks(me), targ_s[part(d), :]).astype(BF16)
        return carry

    lax.fori_loop(0, nsp, pack, 0)
    while m > 1:
        m //= 2
        key_step(m)

    for copy in tot_copies:
        copy.wait_recv()
    offset = jnp.zeros(tot_s.shape, F32)
    for c in range(1, nsq):
        offset = offset + jnp.where(xor(nsq, mine, c) < mine, tot_r[c], 0.0)

    def run_chunk(k, carry):
        def add(j, acc):
            return acc + dot(
                codes_f[:, chunk(j)].astype(BF16), jnp.where(before(j, k), 1.0, 0.0).astype(BF16)
            )

        run = lax.fori_loop(0, nsp, add, jnp.broadcast_to(offset[:, 0:1], (codes_f.shape[0], tok)))
        a_s[k] = jnp.exp(-unit * run)
        b_s[k] = jnp.exp(unit * run)
        return carry

    lax.fori_loop(0, nsp, run_chunk, 0)

    t_copies = {
        c: to_space(t_p.at[xor(nsp, me, c)], t_s.at[me], t_ss, t_rs, c) for c in range(1, nsp)
    }
    for c in reversed(range(1, nsp)):
        x_copies[c].wait_send()
        t_copies[c].start()
    t_s[me] = t_p[me]
    for c in range(1, nsp, 2):
        key_copies[c].wait_recv()

    def flip(i, carry):
        w_t[chunk(i), :] = jnp.transpose(slab[i, 0:state, :].astype(F32)).astype(BF16)
        q_t[chunk(i), :] = jnp.transpose(slab[i, state : 2 * state, :].astype(F32)).astype(BF16)
        return carry

    lax.fori_loop(0, nsp, flip, 0)

    def spread(ref, k):
        t = ref[k]
        return jnp.concatenate(
            [jnp.broadcast_to(t[h : h + 1, :], (width, tok)) for h in range(heads)], axis=0
        )

    def gram(j, k):
        tile = dot(w_t[chunk(j), :], slab[k, state : 2 * state, :])
        return jnp.where(before(j, k), tile, 0.0).astype(BF16)

    whole = gm_c.shape[1] == length

    def columns(k):
        if whole:
            return gm_c[:, chunk(k)]

        def fill(j, carry):
            gm_c[chunk(j), :] = gram(j, k)
            return carry

        lax.fori_loop(0, nsp, fill, 0)
        return gm_c[...]

    def lines(j):
        if whole:
            return gm_c[chunk(j), :]

        def fill(k, carry):
            gm_r[:, chunk(k)] = gram(j, k)
            return carry

        lax.fori_loop(0, nsp, fill, 0)
        return gm_r[...]

    def take_chunk(j, sums, into_t):
        value = x_s[j].astype(F32)
        wide = jnp.concatenate([value * spread(b_s, j), value * spread(a_s, j)], axis=0)
        high = wide.astype(BF16)
        low = (wide - high.astype(F32)).astype(BF16)
        xab[:, chunk(j)] = high
        into = into_t[chunk(j), :]
        return sums + (dot(high, into) + dot(low, into))

    none = jnp.zeros((2 * rows, state), F32)

    def send_states(turn, sums):
        st_s[turn, 0] = sums[0:rows]
        st_s[turn, 1] = sums[rows : 2 * rows]
        copies = []
        for c in range(1, nsq):
            there = xor(nsq, mine, c)
            which = (nsq + mine - there) // nsq
            copies.append(
                to_seq(
                    st_s.at[turn, which], st_r.at[turn, c], st_ss.at[turn], st_rs.at[turn], c
                )
            )
            copies[-1].start()
        return copies

    def take_states(turn, copies, own):
        totals = [jnp.zeros((rows, state), F32), jnp.zeros((rows, state), F32)]
        totals[own] = st_s[turn, own]
        for c in range(1, nsq):
            copies[c - 1].wait_recv()
            got = st_r[turn, c]
            there = xor(nsq, mine, c)
            totals[0] = totals[0] + jnp.where(there < mine, got, 0.0)
            totals[1] = totals[1] + jnp.where(there > mine, got, 0.0)
        for i in range(2):
            high = totals[i].astype(BF16)
            sab[i * rows : (i + 1) * rows, 0:state] = high
            sab[i * rows : (i + 1) * rows, state : 2 * state] = (
                totals[i] - high.astype(F32)
            ).astype(BF16)

    def finish(k, inside, side, own):
        from_k = slab[k, side : side + state, :]
        far = dot(sab[...], jnp.concatenate([from_k, from_k], axis=0))
        signs = (1.0, -1.0) if own == 1 else (-1.0, 1.0)
        out = spread(a_s, k) * (far[0:rows] + signs[0] * inside[0:rows])
        out = out + spread(b_s, k) * (far[rows : 2 * rows] + signs[1] * inside[rows : 2 * rows])
        value = x_s[k].astype(F32)
        skip = jnp.concatenate(
            [value[h * width : (h + 1) * width, :] * gain[h] for h in range(heads)], axis=0
        )
        return (out + skip).astype(BF16)

    def x_chunk(c, sums):
        to_space(feat.at[part(xor(nsp, me, c)), :], x_s.at[me], x_ss, x_rs, c).wait_recv()
        return take_chunk(xor(nsp, me, c), sums, w_t)

    own_x.wait()
    sums = take_chunk(me, none, w_t)
    sums = lax.fori_loop(1, nsp, x_chunk, sums)
    states = send_states(0, sums)
    if whole:

        def fill_all(j, carry):
            def fill(k, carry):
                gm_c[chunk(j), chunk(k)] = gram(j, k)
                return carry

            return lax.fori_loop(0, nsp, fill, carry)

        lax.fori_loop(0, nsp, fill_all, 0)

    take_states(0, states, 1)

    def mixed_copy(c):
        return to_space(mix_s.at[xor(nsp, me, c)], mixed_o.at[part(me), :], m_ss, m_rs, c)

    def forward(i, carry):
        c = nsp - 1 - i
        k = xor(nsp, me, c)
        mix_s[k] = finish(k, dot(xab[...], columns(k)), state, 1)

        @pl.when(c > 0)
        def _():
            mixed_copy(c).start()

        return carry

    lax.fori_loop(0, nsp, forward, 0)
    own_m = pltpu.make_async_copy(mix_s.at[me], mixed_o.at[part(me), :], own_ss.at[2])
    own_m.start()

    def residue(j, sums):
        keep = slab[j, 2 * state : 2 * state + 16, :].astype(F32)[0:1, :]
        wanted = lax.dot_general(
            t_s[j], picks(j), (((0,), (0,)), ((), ())), preferred_element_type=F32
        )
        x_s[j] = (keep * (mix_s[j].astype(F32) - wanted)).astype(BF16)
        return take_chunk(j, sums, q_t)

    def next_residue(c, sums):
        to_space(t_p.at[xor(nsp, me, c)], t_s.at[me], t_ss, t_rs, c).wait_recv()
        return residue(xor(nsp, me, c), sums)

    sums = lax.fori_loop(1, nsp, next_residue, residue(me, none))
    grad_states = send_states(1, sums)
    take_states(1, grad_states, 0)

    def grad_copy(c):
        return to_space(grad_s.at[xor(nsp, me, c)], grad_o.at[part(me), :], g_ss, g_rs, c)

    def backward(i, carry):
        c = nsp - 1 - i
        k = xor(nsp, me, c)
        grad_s[k] = finish(k, dot_nt(xab[...], lines(k)), 0, 0)

        @pl.when(c > 0)
        def _():
            grad_copy(c).start()

        return carry

    lax.fori_loop(0, nsp, backward, 0)
    own_g = pltpu.make_async_copy(grad_s.at[me], grad_o.at[part(me), :], own_ss.at[3])
    own_g.start()

    for c in range(1, nsp):
        key_copies[c].wait_send()
        t_copies[c].wait_send()
    for copies in (tot_copies, states, grad_states):
        for copy in copies:
            copy.wait_send()
    for c in range(1, nsp):
        mixed_copy(c).wait()
        grad_copy(c).wait()
    own_m.wait()
    own_g.wait()


def per_device(
    features, targets, write_keys, read_queries, decay_codes, scan_order, masked, skip_gain
):
    nsp, nsq = lax.axis_size("space"), lax.axis_size("seq")
    heads = decay_codes.shape[0]
    inner, tok = features.shape
    state = write_keys.shape[0]
    length = nsp * tok
    rows = inner // nsp
    unit = 0.065536 / (length * nsq)
    fits = length * length <= 8 * 1024 * 1024
    hp = 16 * (-(-heads // 16))
    vmem = pl.BlockSpec(memory_space=pltpu.VMEM)
    hbm = pl.BlockSpec(memory_space=pl.ANY)
    dma = pltpu.SemaphoreType.DMA
    return pl.pallas_call(
        partial(kernel, nsp, nsq, heads, unit),
        out_shape=(
            jax.ShapeDtypeStruct((inner, tok), BF16), jax.ShapeDtypeStruct((inner, tok), BF16)
        ),
        in_specs=[hbm] * 2 + [vmem] * 5 + [pl.BlockSpec(memory_space=pltpu.SMEM)],
        out_specs=(hbm, hbm),
        scratch_shapes=[
            pltpu.VMEM((nsp, rows, tok), BF16),
            pltpu.VMEM((nsp, masked.shape[0], rows), BF16),
            pltpu.VMEM((nsp, masked.shape[0], rows), BF16),
            pltpu.VMEM((nsp, 2 * state + 16, tok), BF16),
            pltpu.VMEM((2 * rows, length), BF16),
            pltpu.VMEM((nsp, rows, tok), BF16),
            pltpu.VMEM((nsp, rows, tok), BF16),
            pltpu.VMEM((length, length if fits else tok), BF16),
            pltpu.VMEM((16 if fits else tok, length), BF16),
            pltpu.VMEM((length, state), BF16),
            pltpu.VMEM((length, state), BF16),
            pltpu.VMEM((length, 128), F32),
            pltpu.VMEM((nsp, 8, tok), F32),
            pltpu.VMEM((hp, length), F32),
            pltpu.VMEM((nsp, hp, tok), F32),
            pltpu.VMEM((nsp, hp, tok), F32),
            pltpu.VMEM((hp, 128), F32),
            pltpu.VMEM((nsq, hp, 128), F32),
            pltpu.VMEM((2, 2, rows, state), F32),
            pltpu.VMEM((2, nsq, rows, state), F32),
            pltpu.VMEM((2 * rows, 2 * state), BF16),
            *[dma((nsp,)) for _ in range(10)],
            dma((nsq,)), dma((nsq,)),
            dma((2, nsq)), dma((2, nsq)), dma((4,)),
            pltpu.VMEM((inner, tok), BF16),
        ],
        compiler_params=pltpu.CompilerParams(
            collective_id=0, has_side_effects=True, vmem_limit_bytes=56 * 1024 * 1024
        ),
    )(
        features, targets, write_keys, read_queries, decay_codes,
        scan_order.reshape(1, length), masked.reshape(1, masked.shape[0]), skip_gain,
    )


def solution(mesh):
    return jax.shard_map(
        per_device,
        mesh=mesh,
        in_specs=(
            P(None, ("seq", "space")),
            P(None, ("seq", "space")),
            P(None, ("seq", "space")),
            P(None, ("seq", "space")),
            P("space", "seq"),
            P(),
            P(("seq", "space")),
            P("space"),
        ),
        out_specs=(P(None, ("seq", "space")), P(None, ("seq", "space"))),
        check_vma=False,
    )
```
